256 devices in a mesh: grp: 8 (over z_lo, core), lat: 32 (over x, y, z_hi).
Axes of the slice: x: 4, y: 4, z: 8 (z_hi: 2, z_lo: 4; z = z_hi * 4 + z_lo), core: 2. Of those that a mesh axis runs over, the one named last changes fastest.
Arguments:
- spectral_state: bfloat16 [8, 640, 64, 640], P('grp', 'lat'), may hold values from -6 to 6
- cotangent: bfloat16 [8, 640, 64, 640], P('grp', 'lat'), may hold values from -6 to 6
- legendre: bfloat16 [640, 640, 256], P('lat'), as said below
- quadrature: float32 [256], replicated, may hold values from 0.2 to 1
- damping: float32 [32], replicated, may hold values from 0.05 to 20
- physics_in: bfloat16 [512, 32], replicated, may hold values from -1 to 1
- physics_bias: float32 [512], replicated, may hold values from -3 to 3
- physics_out: bfloat16 [32, 512], replicated, may hold values from -0.25 to 0.25
Outputs:
- grad_state: float32 [8, 640, 64, 640], P('grp', 'lat')
- grad_in: float32 [512, 32], replicated
- grad_bias: float32 [512], replicated
- grad_out: float32 [32, 512], replicated
The draws below stay inside these ranges and needn't reach their ends.
Inputs may be any that keep to these rules, and one draw needn't show every extreme that they name: legendre[m, l, p] is zero for every degree l below the wavenumber m, and generally nonzero otherwise.
All inputs are finite; a program needn't handle non-finite values.
Results may differ from the reference program's by a relative error of at most 0.015.
Values may be sent and summed in bfloat16 or wider, within the bound.
A program may use at most 192 MiB of HBM per device.

```python
import math
import jax
import jax.numpy as jnp
from jax import lax

M = 640
L = 640
NLON = 2560
HID = 512
C = 32
NLAT = 256
ROLLOUTS = 8
N_GRP = 8


def draw_legendre(key, part):
    key = jax.random.fold_in(key, 11)
    values = jax.random.uniform(key, (M, L, NLAT), jnp.float32, -1.7320508, 1.7320508)
    wave = jnp.arange(M, dtype=jnp.int32)[:, None]
    degree = jnp.arange(L, dtype=jnp.int32)[None, :]
    live = (degree >= wave).astype(jnp.float32)
    count = (L - jnp.arange(M, dtype=jnp.int32)).astype(jnp.float32)
    scale = 1.0 / jnp.sqrt(count)
    return (values * live[:, :, None] * scale[:, None, None]).astype(jnp.bfloat16)


def block_scale(rng, extent, split, smallest, top_value):
    loudness = 1.0
    for position, parts in split:
        draws = jax.random.uniform(jax.random.fold_in(jax.random.fold_in(rng, 6), position), (parts,), jnp.float32, smallest / len(split), top_value / len(split))
        loudness = loudness * jnp.repeat(jnp.exp(draws), extent[position] // parts).reshape((-1,) + (1,) * (len(extent) - 1 - position))
    return loudness


def centred(stream_key, extent, width, reach, cuts=(), kind=jnp.bfloat16):
    drawn = width * jax.random.normal(stream_key, extent, jnp.float32)
    if cuts:
        drawn = drawn * block_scale(stream_key, extent, cuts, -0.22, 0.18)
    return jnp.clip(drawn, -reach, reach).astype(kind)


def setup_inputs(seed: int = 0) -> dict:
    keys = jax.random.split(jax.random.key(seed), 9)
    return {
        "spectral_state": centred(keys[0], (ROLLOUTS, M, 2 * C, L), 1.0, 6.0, ((0, 8), (1, 32))),
        "cotangent": centred(keys[1], (ROLLOUTS, M, 2 * C, L), 1.0, 6.0, ((0, 8), (1, 32))),
        "legendre": draw_legendre(jax.random.fold_in(keys[8], 71), 0),
        "quadrature": jnp.clip(jax.random.uniform(keys[3], (NLAT,), jnp.float32, 0.2, 1.0), 0.2, 1.0),
        "damping": jnp.clip(jnp.exp(jax.random.uniform(keys[4], (C,), jnp.float32, math.log(0.05), math.log(20.0))), 0.05, 20.0),
        "physics_in": centred(keys[5], (HID, C), C ** -0.5, 1.0),
        "physics_bias": centred(keys[6], (HID,), 0.5, 3.0, (), jnp.float32),
        "physics_out": centred(keys[7], (C, HID), HID ** -0.5, 0.25),
    }


def implicit_factor(damping):
    degree = jnp.arange(L, dtype=jnp.float32)
    ratio = degree * (degree + 1.0) / (L * (L + 1.0))
    factor = 1.0 / (1.0 + damping[:, None] * ratio[None, :])
    return jnp.concatenate([factor, factor], axis=0)

def to_grid(fourier):
    values = fourier.astype(jnp.float32)
    chans = values.shape[1] // 2
    packed = lax.complex(values[:, :chans, :], values[:, chans:, :])
    padded = jnp.zeros((NLON, chans, values.shape[2]), packed.dtype).at[:M].set(packed)
    grid = jnp.real(jnp.fft.ifft(padded, axis=0)) * (NLON * math.sqrt(2.0 / NLON))
    return jnp.transpose(grid, (1, 2, 0))

def from_grid(grid):
    spectrum = jnp.fft.fft(grid, axis=2)[:, :, :M] * math.sqrt(2.0 / NLON)
    stacked = jnp.concatenate([jnp.real(spectrum), jnp.imag(spectrum)], axis=0)
    return jnp.transpose(stacked, (2, 0, 1))

def column_physics(physics_in, physics_bias, physics_out, inputs, tendency):
    hidden = jnp.dot(physics_in, inputs, preferred_element_type=jnp.float32) + physics_bias[:, None]
    sigma = jax.nn.sigmoid(hidden)
    activated = (hidden * sigma).astype(jnp.bfloat16)
    upstream = jnp.dot(physics_out.T, tendency, preferred_element_type=jnp.float32)
    slope = sigma * (1.0 + hidden * (1.0 - sigma))
    pre_grad = (upstream * slope).astype(jnp.bfloat16)
    grad_out = jnp.dot(tendency, activated.T, preferred_element_type=jnp.float32)
    grad_in = jnp.dot(pre_grad, inputs.T, preferred_element_type=jnp.float32)
    grad_bias = lax.optimization_barrier(jnp.sum(pre_grad.astype(jnp.float32), axis=1))
    grid_grad = jnp.dot(physics_in.T, pre_grad, preferred_element_type=jnp.float32).astype(jnp.bfloat16)
    return (grid_grad, grad_in, grad_bias, grad_out)

def reference(spectral_state, cotangent, legendre, quadrature, damping, physics_in, physics_bias, physics_out):
    factor = implicit_factor(damping)
    table = legendre.astype(jnp.float32)

    def one_rollout(pair):
        spectral, cot_in = pair
        direct = cot_in.astype(jnp.float32) * factor[None]
        cot_tend = direct.astype(jnp.bfloat16)
        fourier_state = jnp.einsum('mkl,mlf->mkf', spectral.astype(jnp.float32), table).astype(jnp.bfloat16)
        fourier_cot = (jnp.einsum('mkl,mlf->mkf', cot_tend.astype(jnp.float32), table) * quadrature[None, None, :]).astype(jnp.bfloat16)
        grid_state = to_grid(fourier_state).astype(jnp.bfloat16)
        grid_tend = to_grid(fourier_cot).astype(jnp.bfloat16)

        def per_row(carry, row):
            grid_row, part_in, part_bias, part_out = column_physics(physics_in, physics_bias, physics_out, row[0], row[1])
            return ((carry[0] + part_in, carry[1] + part_bias, carry[2] + part_out), grid_row)
        start = (jnp.zeros((HID, C), jnp.float32), jnp.zeros((HID,), jnp.float32), jnp.zeros((C, HID), jnp.float32))
        sums, rows = lax.scan(per_row, start, (jnp.transpose(grid_state, (1, 0, 2)), jnp.transpose(grid_tend, (1, 0, 2))))
        grid_grad = jnp.transpose(rows, (1, 0, 2))
        fourier_grad = from_grid(grid_grad.astype(jnp.float32)).astype(jnp.bfloat16)
        grad_state = direct + jnp.einsum('mkf,mlf->mkl', fourier_grad.astype(jnp.float32), table)
        return (grad_state, sums[0], sums[1], sums[2])
    grad_state, grad_in, grad_bias, grad_out = lax.map(one_rollout, (spectral_state, cotangent))
    scale = 1.0 / math.sqrt(N_GRP * NLAT * NLON)
    return (grad_state, lax.optimization_barrier(jnp.sum(grad_in, axis=0)) * scale, lax.optimization_barrier(jnp.sum(grad_bias, axis=0)) * scale, lax.optimization_barrier(jnp.sum(grad_out, axis=0)) * scale)
```

```python
import functools
import math

import jax
import jax.numpy as jnp
import ml_dtypes
import numpy as np
from jax import lax
from jax.experimental import pallas as pl
from jax.experimental.pallas import tpu as pltpu
from jax.sharding import PartitionSpec as P

NLON = 2560
HALF = NLON // 2
MESH = pl.DeviceIdType.MESH
F32, BF16 = jnp.float32, jnp.bfloat16

LAT = 32
GRP = 8
XY = 16
MB = 20
HB = MB // 2
NL = 640
NP = 256
CH = 32
HID = 512
COLS = 640
JT = 640
SEND = ((0, 48), (48, 80), (80, 128), (128, 160))
BACK = ((0, 32), (32, 48), (48, 80))
GR = 17


def table_rows(e):
    if e < 8:
        base = 256 * (e // 4) + LAT * (e % 4)
        return base, base + 128
    return 512 + LAT * (e - 8), 576 + LAT * (e - 8)


def longitude_tables():
    place = np.arange(HALF, dtype=np.int64)[:, None]
    owner = np.arange(LAT, dtype=np.int64)[None, :]
    tables = np.zeros((2, HALF, COLS), np.float64)
    scale = math.sqrt(2.0 / NLON)
    for parity in range(2):
        for e in range(HB):
            wave = MB * owner + 2 * e + parity
            angle = (wave * place % NLON) * (2.0 * math.pi / NLON)
            c, s = table_rows(e)
            tables[parity, :, c : c + LAT] = np.cos(angle) * scale
            tables[parity, :, s : s + LAT] = -np.sin(angle) * scale
    return tables.astype(ml_dtypes.bfloat16)


def dot(a, b, ca, cb):
    return lax.dot_general(a, b, (((ca,), (cb,)), ((), ())), preferred_element_type=F32)


def kernel(
    spec_hbm, cot_hbm, leg_hbm, tab_hbm, quad_ref, damp_ref, pin_ref, bias_ref, pout_ref,
    out_hbm, og_ref, ob_ref,
    spec, cot, leg, tab, factor, ft, stage, snd, rcv, rf, wdft, wp, w1t, racc, rall, bsnd, brcv,
    gp, ga, gsnd, g1, g2s, g2r, g3s, g3r, g4s, g4r, outb,
    in_sem, tab_sem, f_s, f_r, b_s, b_r, g_s, g_r, out_sem,
):
    me = lax.axis_index("lat")
    grp = lax.axis_index("grp")
    xy = me // 2

    def peer(k):
        return lax.rem(me + k, LAT)

    barrier = pltpu.get_barrier_semaphore()

    @pl.loop(1, LAT)
    def _(k):
        pl.semaphore_signal(barrier, inc=1, device_id={"lat": peer(k)}, device_id_type=MESH)

    @pl.loop(1, GRP)
    def _(k):
        pl.semaphore_signal(
            barrier, inc=1, device_id={"grp": lax.rem(grp + k, GRP)}, device_id_type=MESH
        )

    def wave(mm):
        return 2 * lax.rem(mm, HB) + mm // HB

    def loads(mm):
        m = wave(mm)
        return [
            pltpu.make_async_copy(src.at[m], dst.at[m], in_sem.at[i, mm])
            for i, (src, dst) in enumerate(((spec_hbm, spec), (cot_hbm, cot), (leg_hbm, leg)))
        ]

    @pl.loop(0, MB)
    def _(mm):
        for copy in loads(mm):
            copy.start()

    tab_copy = pltpu.make_async_copy(tab_hbm, tab, tab_sem)
    tab_copy.start()

    degree = lax.broadcasted_iota(jnp.int32, (CH, NL), 1).astype(F32)
    ratio = degree * (degree + 1.0) / (NL * (NL + 1.0))
    factor[...] = 1.0 / (1.0 + damp_ref[...] * ratio)

    @pl.loop(0, MB)
    def _(mm):
        m = wave(mm)
        for copy in loads(mm):
            copy.wait()
        fac = factor[...]
        s = spec[m]
        c = cot[m].astype(F32)
        c_re = (c[:CH] * fac).astype(BF16)
        c_im = (c[CH:] * fac).astype(BF16)
        lhs = jnp.concatenate([s[:CH], c_re, s[CH:], c_im], axis=0)
        four = dot(lhs, leg[m], 1, 0)
        quad = quad_ref[...]
        four = jnp.concatenate(
            [four[:32], four[32:64] * quad, four[64:96], four[96:] * quad], axis=0
        )
        ft[pl.ds(pl.multiple_of(mm * NP, NP), NP), :] = four.T

    pl.semaphore_wait(barrier, LAT - 1 + GRP - 1)

    def assemble(pair, d):
        for j in range(4):
            row = 128 * (j % 2) + 32 * (2 * pair + j // 2) + d
            stage[pl.ds(MB * j, MB), :] = ft[pl.ds(row, MB, stride=NP), :]
        snd[d, pl.ds(80 * pair, 80), :] = stage[...].astype(BF16)

    def send(c, d):
        lo, hi = SEND[c]
        pltpu.make_async_remote_copy(
            src_ref=snd.at[d, pl.ds(lo, hi - lo)],
            dst_ref=rcv.at[me, pl.ds(lo, hi - lo)],
            send_sem=f_s.at[c],
            recv_sem=f_r.at[c],
            device_id={"lat": d},
            device_id_type=MESH,
        ).start()

    def keep(c):
        lo, hi = SEND[c]
        pltpu.make_async_copy(
            snd.at[me, pl.ds(lo, hi - lo)], rcv.at[me, pl.ds(lo, hi - lo)], f_r.at[c]
        ).start()

    def far_then_near(f):
        @pl.loop(0, LAT // 2)
        def _(i):
            f(peer(2 * i + 1))

        @pl.loop(1, LAT // 2)
        def _(i):
            f(peer(2 * i))

    def pack_send(pair, c):
        def f(d):
            assemble(pair, d)
            send(c, d)

        return f

    far_then_near(pack_send(0, 0))
    assemble(0, me)
    keep(0)
    far_then_near(functools.partial(send, 1))
    keep(1)

    @pl.loop(0, LAT)
    def _(d):
        assemble(1, d)

    wp[...] = jnp.zeros_like(wp)
    w_in = pin_ref[...].astype(F32).T
    w1t[...] = w_in.astype(BF16)
    half_in = (0.5 * w_in).astype(BF16)
    half_out = (0.5 * pout_ref[...].astype(F32)).astype(BF16)
    half_bias = 0.5 * bias_ref[...]
    top = half_bias.astype(BF16).astype(F32)
    mid = (half_bias - top).astype(BF16).astype(F32)
    low = half_bias - top - mid
    row = lax.broadcasted_iota(jnp.int32, (16, HID), 0)
    bias_rows = jnp.where(
        row == 0, top, jnp.where(row == 1, mid, jnp.where(row == 2, low, 0.0))
    ).astype(BF16)
    for s in range(2):
        wp[s, pl.ds(64 * s, CH), pl.ds(0, HID)] = half_in
        wp[s, pl.ds(64 * s + CH, CH), pl.ds(HID, HID)] = half_out
        wp[s, pl.ds(128, 16), pl.ds(0, HID)] = bias_rows
    gp[...] = jnp.zeros_like(gp)
    ga[...] = jnp.zeros_like(ga)
    tab_copy.wait()

    lane = lax.broadcasted_iota(jnp.int32, (LAT, 128), 1)
    left = lane < 64

    def arrive(c):
        lo, hi = SEND[c]
        span = rcv.at[:, pl.ds(lo, hi - lo)]
        pltpu.make_async_copy(span, span, f_r.at[c]).wait()

        at = lo % 80

        @pl.loop(0, LAT)
        def _(src):
            rf[pl.ds(pl.multiple_of(src * 80 + at, 8), hi - lo), :] = rcv[
                src, pl.ds(lo, hi - lo), :
            ].astype(F32)

        first = 40 * (c % 2)
        for mm in range(MB):
            w0 = rf[pl.ds(first + mm, LAT, stride=80), :]
            w1 = rf[pl.ds(first + MB + mm, LAT, stride=80), :]
            re = jnp.where(left, w0, pltpu.roll(w1, 64, 1))
            im = jnp.where(left, pltpu.roll(w0, 64, 1), w1)
            r_re, r_im = table_rows(mm % HB)
            wdft[mm // HB, pl.ds(r_re, LAT), :] = re.astype(BF16)
            wdft[mm // HB, pl.ds(r_im, LAT), :] = im.astype(BF16)

    one_lane = lax.broadcasted_iota(jnp.int32, (2 * JT, 128), 1)
    ones = jnp.where(one_lane < 3, 1.0, 0.0).astype(BF16)
    ones_t = jnp.ones((16, 2 * JT), BF16)

    def physics(i, _):
        span = pl.ds(pl.multiple_of(i * JT, JT), JT)
        even = dot(tab[0, span, :], wdft[0], 1, 0)
        odd = dot(tab[1, span, :], wdft[1], 1, 0)
        x = jnp.concatenate([(even + odd).astype(BF16), (even - odd).astype(BF16)], axis=0)
        xe = jnp.concatenate([x, ones], axis=1)
        xt = x.T
        grads = []
        for s in range(2):
            h = dot(xe, wp[s, :, pl.ds(0, HID)], 1, 0)
            u = dot(xe, wp[s, :, pl.ds(HID, HID)], 1, 0)
            a = 1.0 + jnp.tanh(h)
            act = h * a
            pre = (u * (a * ((1.0 + (h + h)) - act))).astype(BF16)
            act = act.astype(BF16)
            grads.append(dot(w1t[...], pre, 1, 1))
            lhs = jnp.concatenate([xt[64 * s : 64 * s + CH], ones_t], axis=0)
            gp[...] += dot(lhs, pre, 1, 0)
            ga[...] += dot(xt[64 * s + CH : 64 * s + 64], act, 1, 0)
        gg = jnp.concatenate(grads, axis=0)
        g_even = (gg[:, :JT] + gg[:, JT:]).astype(BF16)
        g_odd = (gg[:, :JT] - gg[:, JT:]).astype(BF16)
        racc[0] += dot(g_even, tab[0, span, :], 1, 0)
        racc[1] += dot(g_odd, tab[1, span, :], 1, 0)
        return 0

    def turn(c):
        for parity in range(2):
            r = racc[parity]
            base = 640 * c + 320 * parity
            rall[pl.ds(base, 128), :] = jnp.concatenate([r[:, :128], r[:, 128:256]], axis=0).T
            rall[pl.ds(base + 128, 128), :] = jnp.concatenate(
                [r[:, 256:384], r[:, 384:512]], axis=0
            ).T
            last = r[:, 512:]
            both = jnp.concatenate([last, pltpu.roll(last, 64, 1)], axis=0).T
            rall[pl.ds(base + 256, 64), :] = both[:64]

    def back(n):
        lo, hi = BACK[n]
        first = lo // MB
        last = (hi - 1) // MB

        def pack(d):
            for q in range(first, last + 1):
                stage[pl.ds(MB * q, MB), :] = rall[pl.ds(640 * q + d, MB, stride=LAT), :]
            bsnd[d, pl.ds(lo, hi - lo), :] = stage[pl.ds(lo, hi - lo), :].astype(BF16)

        def go(d):
            pack(d)
            pltpu.make_async_remote_copy(
                src_ref=bsnd.at[d, pl.ds(lo, hi - lo)],
                dst_ref=brcv.at[me, pl.ds(lo, hi - lo)],
                send_sem=b_s.at[n],
                recv_sem=b_r.at[n],
                device_id={"lat": d},
                device_id_type=MESH,
            ).start()

        far_then_near(go)
        pack(me)
        pltpu.make_async_copy(
            bsnd.at[me, pl.ds(lo, hi - lo)], brcv.at[me, pl.ds(lo, hi - lo)], b_r.at[n]
        ).start()

    def xy_step(n, src, dst, mine):
        @pl.loop(1, XY)
        def _(i):
            d = peer(2 * i)
            pltpu.make_async_remote_copy(
                src_ref=src(d // 2),
                dst_ref=dst.at[xy],
                send_sem=g_s.at[n],
                recv_sem=g_r.at[n],
                device_id={"lat": d},
                device_id_type=MESH,
            ).start()

        pltpu.make_async_copy(src(mine), dst.at[xy], g_r.at[n]).start()

    def reduce_1():
        for e in range(XY):
            block, tile = e // 4, e % 4
            cols = pl.ds(128 * tile, 128)
            if block < 2:
                gsnd[e, pl.ds(0, 16), :] = gp[pl.ds(16 * block, 16), cols]
            else:
                gsnd[e, pl.ds(0, 16), :] = ga[pl.ds(16 * (block - 2), 16), cols]
            gsnd[e, pl.ds(16, 1), :] = gp[pl.ds(CH, 1), cols]
        xy_step(0, lambda e: gsnd.at[e], g1, xy)

    def reduce_2():
        pltpu.make_async_copy(g1, g1, g_r.at[0]).wait()
        total = g1[0]
        for e in range(1, XY):
            total = total + g1[e]
        g2s[...] = total
        copy = pltpu.make_async_remote_copy(
            src_ref=g2s,
            dst_ref=g2r,
            send_sem=g_s.at[1],
            recv_sem=g_r.at[1],
            device_id={"lat": me + 1 - 2 * lax.rem(me, 2)},
            device_id_type=MESH,
        )
        copy.start()

    def reduce_3():
        pltpu.make_async_copy(g2r, g2r, g_r.at[1]).wait()
        g3s[...] = g2s[...] + g2r[...]

        @pl.loop(1, GRP)
        def _(k):
            pltpu.make_async_remote_copy(
                src_ref=g3s,
                dst_ref=g3r.at[grp],
                send_sem=g_s.at[2],
                recv_sem=g_r.at[2],
                device_id={"grp": lax.rem(grp + k, GRP)},
                device_id_type=MESH,
            ).start()

        pltpu.make_async_copy(g3s, g3r.at[grp], g_r.at[2]).start()

    def reduce_4():
        pltpu.make_async_copy(g3r, g3r, g_r.at[2]).wait()
        total = g3r[0]
        for e in range(1, GRP):
            total = total + g3r[e]
        g4s[...] = total
        xy_step(3, lambda e: g4s, g4r, xy)

    def reduce_5():
        pltpu.make_async_copy(g4r, g4r, g_r.at[3]).wait()
        for e in range(XY):
            block, tile = e // 4, e % 4
            cols = pl.ds(128 * tile, 128)
            og_ref[pl.ds(16 * block, 16), cols] = g4r[e, pl.ds(0, 16), :]
            if block == 0:
                ob_ref[:, cols] = g4r[e, pl.ds(16, 1), :]

    @pl.loop(0, 4)
    def _(c):
        for now in range(4):

            @pl.when(c == now)
            def _():
                arrive(now)
                if now < 2:
                    far_then_near(functools.partial(send, now + 2))
                    keep(now + 2)

        racc[...] = jnp.zeros_like(racc)
        lax.fori_loop(0, HALF // JT, physics, 0)
        for now in range(4):

            @pl.when(c == now)
            def _():
                if now == 3:
                    reduce_1()
                turn(now)
                if now > 0:
                    back(now - 1)

    def unpack(n):
        lo, hi = BACK[n]
        span = brcv.at[:, pl.ds(lo, hi - lo)]
        pltpu.make_async_copy(span, span, b_r.at[n]).wait()

        @pl.loop(0, LAT)
        def _(src):
            rf[pl.ds(pl.multiple_of(src * 80 + lo, 8), hi - lo), :] = brcv[
                src, pl.ds(lo, hi - lo), :
            ].astype(F32)

    def inverse(mm, _):
        m = wave(mm)
        rows = jnp.concatenate(
            [rf[pl.ds(MB * q + mm, LAT, stride=80), :] for q in range(4)], axis=0
        )
        t = rows.T.astype(BF16)
        lhs = jnp.concatenate(
            [
                jnp.concatenate([t[:32], t[64:96]], axis=0),
                jnp.concatenate([t[32:64], t[96:]], axis=0),
            ],
            axis=1,
        )
        fac = factor[...]
        direct = cot[m].astype(F32) * jnp.concatenate([fac, fac], axis=0)
        outb[m] = direct + dot(lhs, leg[m], 1, 1)
        pltpu.make_async_copy(outb.at[m], out_hbm.at[m], out_sem).start()
        return 0

    unpack(0)
    unpack(1)
    reduce_2()
    reduce_3()
    unpack(2)
    reduce_4()
    lax.fori_loop(0, MB, inverse, 0)
    reduce_5()

    pltpu.make_async_copy(outb, out_hbm, out_sem).wait()
    for c, (lo, hi) in enumerate(SEND):
        span = snd.at[pl.ds(0, LAT - 1), pl.ds(lo, hi - lo)]
        pltpu.make_async_copy(span, span, f_s.at[c]).wait()
    for n, (lo, hi) in enumerate(BACK):
        span = bsnd.at[pl.ds(0, LAT - 1), pl.ds(lo, hi - lo)]
        pltpu.make_async_copy(span, span, b_s.at[n]).wait()
    for n, count, buf in ((0, XY - 1, g1), (2, GRP - 1, g3r), (3, XY - 1, g4r)):
        span = buf.at[pl.ds(0, count)]
        pltpu.make_async_copy(span, span, g_s.at[n]).wait()
    pltpu.make_async_copy(g2s, g2s, g_s.at[1]).wait()


def body(
    tables,
    spectral_state, cotangent, legendre, quadrature, damping, physics_in, physics_bias, physics_out,
):
    hbm = pl.BlockSpec(memory_space=pl.ANY)
    vmem = pl.BlockSpec(memory_space=pltpu.VMEM)
    dma = pltpu.SemaphoreType.DMA
    scratch = [
        pltpu.VMEM((MB, 2 * CH, NL), BF16),
        pltpu.VMEM((MB, 2 * CH, NL), BF16),
        pltpu.VMEM((MB, NL, NP), BF16),
        pltpu.VMEM((2, HALF, COLS), BF16),
        pltpu.VMEM((CH, NL), F32),
        pltpu.VMEM((MB * NP, 128), F32),
        pltpu.VMEM((80, 128), F32),
        pltpu.VMEM((LAT, 160, 128), BF16),
        pltpu.VMEM((LAT, 160, 128), BF16),
        pltpu.VMEM((LAT * 80, 128), F32),
        pltpu.VMEM((2, COLS, 128), BF16),
        pltpu.VMEM((2, 256, 2 * HID), BF16),
        pltpu.VMEM((CH, HID), BF16),
        pltpu.VMEM((2, 64, COLS), F32),
        pltpu.VMEM((4 * 640, 128), F32),
        pltpu.VMEM((LAT, 80, 128), BF16),
        pltpu.VMEM((LAT, 80, 128), BF16),
        pltpu.VMEM((48, HID), F32),
        pltpu.VMEM((CH, HID), F32),
        pltpu.VMEM((XY, GR, 128), F32),
        pltpu.VMEM((XY, GR, 128), F32),
        pltpu.VMEM((GR, 128), F32),
        pltpu.VMEM((GR, 128), F32),
        pltpu.VMEM((GR, 128), F32),
        pltpu.VMEM((GRP, GR, 128), F32),
        pltpu.VMEM((GR, 128), F32),
        pltpu.VMEM((XY, GR, 128), F32),
        pltpu.VMEM((MB, 2 * CH, NL), F32),
        dma((3, MB)),
        dma,
        dma((4,)),
        dma((4,)),
        dma((3,)),
        dma((3,)),
        dma((4,)),
        dma((4,)),
        dma,
    ]
    grad_state, grads, grad_bias = pl.pallas_call(
        kernel,
        out_shape=[
            jax.ShapeDtypeStruct((MB, 2 * CH, NL), F32),
            jax.ShapeDtypeStruct((2 * CH, HID), F32),
            jax.ShapeDtypeStruct((1, HID), F32),
        ],
        in_specs=[hbm] * 4 + [vmem] * 5,
        out_specs=[hbm, vmem, vmem],
        scratch_shapes=scratch,
        compiler_params=pltpu.CompilerParams(
            collective_id=0, has_side_effects=True, vmem_limit_bytes=60 * 2**20
        ),
    )(
        spectral_state[0],
        cotangent[0],
        legendre,
        tables,
        quadrature[None, :],
        damping[:, None],
        physics_in,
        physics_bias[None, :],
        physics_out,
    )
    scale = 1.0 / math.sqrt(GRP * NP * NLON)
    return (grad_state[None], grads[:CH].T * scale, grad_bias[0] * scale, grads[CH:] * scale)


def solution(mesh):
    in_specs = (
        P(),
        P("grp", "lat", None, None),
        P("grp", "lat", None, None),
        P("lat", None, None),
        P(),
        P(),
        P(),
        P(),
        P(),
    )
    out_specs = (P("grp", "lat", None, None), P(), P(), P())
    mapped = jax.shard_map(body, mesh=mesh, in_specs=in_specs, out_specs=out_specs, check_vma=False)
    tables = longitude_tables()

    def run(*args):
        return mapped(jnp.asarray(tables), *args)

    return run
```

```python
import functools
import math

import jax
import jax.numpy as jnp
import ml_dtypes
import numpy as np
from jax import lax
from jax.experimental import pallas as pl
from jax.experimental.pallas import tpu as pltpu
from jax.sharding import PartitionSpec as P

NLON = 2560
HALF = NLON // 2
MESH = pl.DeviceIdType.MESH
F32, BF16 = jnp.float32, jnp.bfloat16

LAT = 32
GRP = 8
XY = 16
MB = 20
HB = MB // 2
NL = 640
NP = 256
CH = 32
HID = 512
COLS = 640
JT = 640
SEND = ((0, 16), (16, 32), (32, 48), (48, 80), (80, 128), (128, 160))
ARRIVE = ((0, 1, 2), (3,), (4,), (5,))
BACK = ((0, 32), (32, 48), (48, 80))
GR = 17
STEP = 4
VMEM_LIMIT = 44 * 2**20


def table_rows(e):
    if e < 8:
        base = 256 * (e // 4) + LAT * (e % 4)
        return base, base + 128
    return 512 + LAT * (e - 8), 576 + LAT * (e - 8)


def longitude_tables():
    place = np.arange(HALF, dtype=np.int64)[:, None]
    owner = np.arange(LAT, dtype=np.int64)[None, :]
    tables = np.zeros((2, HALF, COLS), np.float64)
    scale = math.sqrt(2.0 / NLON)
    for parity in range(2):
        for e in range(HB):
            wave = MB * owner + 2 * e + parity
            angle = (wave * place % NLON) * (2.0 * math.pi / NLON)
            c, s = table_rows(e)
            tables[parity, :, c : c + LAT] = np.cos(angle) * scale
            tables[parity, :, s : s + LAT] = -np.sin(angle) * scale
    return tables.astype(ml_dtypes.bfloat16)


def dot(a, b, ca, cb):
    return lax.dot_general(a, b, (((ca,), (cb,)), ((), ())), preferred_element_type=F32)


def implicit_factor(damping):
    across = lax.broadcasted_iota(jnp.int32, (CH, CH), 0)
    along = lax.broadcasted_iota(jnp.int32, (CH, CH), 1)
    column = jnp.sum(jnp.where(across == along, damping, 0.0), axis=1, keepdims=True)
    degree = lax.broadcasted_iota(jnp.int32, (CH, NL), 1).astype(F32)
    ratio = degree * (degree + 1.0) / (NL * (NL + 1.0))
    return 1.0 / (1.0 + column * ratio)


def inverse_kernel(a_ref, cot_ref, leg_ref, damp_ref, gr_ref, out_ref, gi_ref, gb_ref, go_ref, fac):
    @pl.when(pl.program_id(0) == 0)
    def _():
        factor = implicit_factor(damp_ref[...])
        fac[...] = jnp.concatenate([factor, factor], axis=0)
        scale = 1.0 / math.sqrt(GRP * NP * NLON)
        for e in range(XY):
            block, tile = e // 4, e % 4
            cols = pl.ds(128 * tile, 128)
            piece = gr_ref[e, pl.ds(0, 16), :] * scale
            if block < 2:
                gi_ref[pl.ds(16 * block, 16), cols] = piece
            else:
                go_ref[pl.ds(16 * (block - 2), 16), cols] = piece
            if block == 0:
                gb_ref[:, cols] = gr_ref[e, pl.ds(16, 1), :] * scale

    for i in range(STEP):
        out_ref[i] = cot_ref[i].astype(F32) * fac[...] + dot(a_ref[i], leg_ref[i], 1, 1)


def kernel(
    spec_hbm, cot_hbm, leg_hbm, tab_hbm, quad_ref, damp_ref, pin_ref, bias_ref, pout_ref,
    a_ref, gr_ref,
    spec, cot, leg, tab, factor, ft, stage, snd, rcv, rf, wdft, wp, racc, rall, bsnd, brcv,
    gp, ga, gsnd, g1, g2s, g2r, g3s, g3r, g4s, g4r,
    in_sem, tab_sem, f_s, f_r, b_s, b_r, g_s, g_r,
):
    me = lax.axis_index("lat")
    grp = lax.axis_index("grp")
    xy = me // 2

    def peer(k):
        return lax.rem(me + k, LAT)

    barrier = pltpu.get_barrier_semaphore()

    @pl.loop(1, LAT)
    def _(k):
        pl.semaphore_signal(barrier, inc=1, device_id={"lat": peer(k)}, device_id_type=MESH)

    @pl.loop(1, GRP)
    def _(k):
        pl.semaphore_signal(
            barrier, inc=1, device_id={"grp": lax.rem(grp + k, GRP)}, device_id_type=MESH
        )

    def wave(mm):
        return 2 * lax.rem(mm, HB) + mm // HB

    def loads(mm):
        m = wave(mm)
        return [
            pltpu.make_async_copy(src.at[m], dst.at[m], in_sem.at[i, mm])
            for i, (src, dst) in enumerate(((spec_hbm, spec), (cot_hbm, cot), (leg_hbm, leg)))
        ]

    @pl.loop(0, MB)
    def _(mm):
        for copy in loads(mm):
            copy.start()

    tab_copy = pltpu.make_async_copy(tab_hbm, tab, tab_sem)
    tab_copy.start()

    factor[...] = implicit_factor(damp_ref[...])

    def legendre(mm):
        m = wave(mm)
        for copy in loads(mm):
            copy.wait()
        fac = factor[...]
        s = spec[m]
        c = cot[m].astype(F32)
        c_re = (c[:CH] * fac).astype(BF16)
        c_im = (c[CH:] * fac).astype(BF16)
        lhs = jnp.concatenate([s[:CH], c_re, s[CH:], c_im], axis=0)
        four = dot(lhs, leg[m], 1, 0)
        quad = quad_ref[...]
        four = jnp.concatenate(
            [four[:32], four[32:64] * quad, four[64:96], four[96:] * quad], axis=0
        )
        ft[pl.ds(pl.multiple_of(mm * NP, NP), NP), :] = four.T

    def tile(q, t, d):
        rows = [
            ft[pl.ds(8 * t * NP + 128 * half + 32 * q + d, 8, stride=NP), :] for half in range(2)
        ]
        return jnp.concatenate(rows, axis=0).astype(BF16)

    def rest(pair, d):
        for j in range(4):
            row = 16 * NP + 128 * (j % 2) + 32 * (2 * pair + j // 2) + d
            stage[pl.ds(4 * j, 4), :] = ft[pl.ds(row, 4, stride=NP), :]
        return stage[pl.ds(0, 16), :].astype(BF16)

    def assemble(n, d):
        if n < 2:
            snd[d, pl.ds(16 * n, 16), :] = tile(0, n, d)
        elif n == 2:
            snd[d, pl.ds(32, 16), :] = rest(0, d)
        elif n == 3:
            for t in range(2):
                snd[d, pl.ds(48 + 16 * t, 16), :] = tile(1, t, d)
        elif n == 4:
            for t in range(2):
                snd[d, pl.ds(80 + 16 * t, 16), :] = tile(2, t, d)
            snd[d, pl.ds(112, 16), :] = rest(1, d)
        else:
            for t in range(2):
                snd[d, pl.ds(128 + 16 * t, 16), :] = tile(3, t, d)

    def send(n, d):
        lo, hi = SEND[n]
        pltpu.make_async_remote_copy(
            src_ref=snd.at[d, pl.ds(lo, hi - lo)],
            dst_ref=rcv.at[me, pl.ds(lo, hi - lo)],
            send_sem=f_s.at[n],
            recv_sem=f_r.at[n],
            device_id={"lat": d},
            device_id_type=MESH,
        ).start()

    def far_then_near(f):
        @pl.loop(0, LAT // 2)
        def _(i):
            f(peer(2 * i + 1))

        @pl.loop(1, LAT // 2)
        def _(i):
            f(peer(2 * i))

    def forward(n, ready=False):
        def f(d):
            if not ready:
                assemble(n, d)
            send(n, d)

        far_then_near(f)
        if not ready:
            assemble(n, me)
        lo, hi = SEND[n]
        pltpu.make_async_copy(
            snd.at[me, pl.ds(lo, hi - lo)], rcv.at[me, pl.ds(lo, hi - lo)], f_r.at[n]
        ).start()

    pl.loop(0, 8)(legendre)
    pl.semaphore_wait(barrier, LAT - 1 + GRP - 1)
    forward(0)
    pl.loop(8, 16)(legendre)
    forward(1)
    pl.loop(16, MB)(legendre)
    forward(2)
    forward(3)

    @pl.loop(0, LAT)
    def _(d):
        assemble(4, d)
        assemble(5, d)

    wp[...] = jnp.zeros_like(wp)
    half_in = (0.5 * pin_ref[...].astype(F32)).astype(BF16)
    half_out = (0.5 * pout_ref[...].astype(F32)).astype(BF16)
    half_bias = 0.5 * bias_ref[...]
    top = half_bias.astype(BF16).astype(F32)
    mid = (half_bias - top).astype(BF16).astype(F32)
    low = half_bias - top - mid
    row = lax.broadcasted_iota(jnp.int32, (16, HID), 0)
    bias_rows = jnp.where(
        row == 0, top, jnp.where(row == 1, mid, jnp.where(row == 2, low, 0.0))
    ).astype(BF16)
    for s in range(2):
        wp[s, pl.ds(64 * s, CH), pl.ds(0, HID)] = half_in
        wp[s, pl.ds(64 * s + CH, CH), pl.ds(HID, HID)] = half_out
        wp[s, pl.ds(128, 16), pl.ds(0, HID)] = bias_rows
    gp[...] = jnp.zeros_like(gp)
    ga[...] = jnp.zeros_like(ga)
    tab_copy.wait()

    lane = lax.broadcasted_iota(jnp.int32, (LAT, 128), 1)
    left = lane < 64

    def arrive(c):
        for n in ARRIVE[c]:
            lo, hi = SEND[n]
            span = rcv.at[:, pl.ds(lo, hi - lo)]
            pltpu.make_async_copy(span, span, f_r.at[n]).wait()
            at = lo % 80

            @pl.loop(0, LAT)
            def _(src):
                rf[pl.ds(pl.multiple_of(src * 80 + at, 8), hi - lo), :] = rcv[
                    src, pl.ds(lo, hi - lo), :
                ].astype(F32)

        def row(half, mm):
            if mm < 16:
                return 48 * (c % 2) + 16 * (mm // 8) + 8 * half + mm % 8
            return 32 + 8 * (c % 2) + 4 * half + mm - 16

        for mm in range(MB):
            w0 = rf[pl.ds(row(0, mm), LAT, stride=80), :]
            w1 = rf[pl.ds(row(1, mm), LAT, stride=80), :]
            re = jnp.where(left, w0, pltpu.roll(w1, 64, 1))
            im = jnp.where(left, pltpu.roll(w0, 64, 1), w1)
            r_re, r_im = table_rows(mm % HB)
            wdft[mm // HB, pl.ds(r_re, LAT), :] = re.astype(BF16)
            wdft[mm // HB, pl.ds(r_im, LAT), :] = im.astype(BF16)

    one_lane = lax.broadcasted_iota(jnp.int32, (2 * JT, 128), 1)
    ones = jnp.where(one_lane < 3, 1.0, 0.0).astype(BF16)
    ones_t = jnp.ones((16, 2 * JT), BF16)

    def physics(i, _):
        span = pl.ds(pl.multiple_of(i * JT, JT), JT)
        even = dot(tab[0, span, :], wdft[0], 1, 0)
        odd = dot(tab[1, span, :], wdft[1], 1, 0)
        x = jnp.concatenate([(even + odd).astype(BF16), (even - odd).astype(BF16)], axis=0)
        xe = jnp.concatenate([x, ones], axis=1)
        xt = x.T
        grads = []
        for s in range(2):
            h = dot(xe, wp[s, :, pl.ds(0, HID)], 1, 0)
            u = dot(xe, wp[s, :, pl.ds(HID, HID)], 1, 0)
            a = 1.0 + jnp.tanh(h)
            act = h * a
            pre = (u * (a * ((1.0 + (h + h)) - act))).astype(BF16)
            act = act.astype(BF16)
            grads.append(dot(pin_ref[...], pre, 1, 1))
            lhs = jnp.concatenate([xt[64 * s : 64 * s + CH], ones_t], axis=0)
            gp[...] += dot(lhs, pre, 1, 0)
            ga[...] += dot(xt[64 * s + CH : 64 * s + 64], act, 1, 0)
        gg = jnp.concatenate(grads, axis=0)
        g_even = (gg[:, :JT] + gg[:, JT:]).astype(BF16)
        g_odd = (gg[:, :JT] - gg[:, JT:]).astype(BF16)
        racc[0] += dot(g_even, tab[0, span, :], 1, 0)
        racc[1] += dot(g_odd, tab[1, span, :], 1, 0)
        return 0

    def turn(c):
        for parity in range(2):
            r = racc[parity]
            base = 640 * c + 320 * parity
            rall[pl.ds(base, 128), :] = jnp.concatenate([r[:, :128], r[:, 128:256]], axis=0).T
            rall[pl.ds(base + 128, 128), :] = jnp.concatenate(
                [r[:, 256:384], r[:, 384:512]], axis=0
            ).T
            last = r[:, 512:]
            both = jnp.concatenate([last, pltpu.roll(last, 64, 1)], axis=0).T
            rall[pl.ds(base + 256, 64), :] = both[:64]

    def back(n):
        lo, hi = BACK[n]
        first = lo // MB
        last = (hi - 1) // MB

        def pack(d):
            for q in range(first, last + 1):
                stage[pl.ds(MB * q, MB), :] = rall[pl.ds(640 * q + d, MB, stride=LAT), :]
            bsnd[d, pl.ds(lo, hi - lo), :] = stage[pl.ds(lo, hi - lo), :].astype(BF16)

        def go(d):
            pack(d)
            pltpu.make_async_remote_copy(
                src_ref=bsnd.at[d, pl.ds(lo, hi - lo)],
                dst_ref=brcv.at[me, pl.ds(lo, hi - lo)],
                send_sem=b_s.at[n],
                recv_sem=b_r.at[n],
                device_id={"lat": d},
                device_id_type=MESH,
            ).start()

        far_then_near(go)
        pack(me)
        pltpu.make_async_copy(
            bsnd.at[me, pl.ds(lo, hi - lo)], brcv.at[me, pl.ds(lo, hi - lo)], b_r.at[n]
        ).start()

    def xy_step(n, src, dst, mine):
        @pl.loop(1, XY)
        def _(i):
            d = peer(2 * i)
            pltpu.make_async_remote_copy(
                src_ref=src(d // 2),
                dst_ref=dst.at[xy],
                send_sem=g_s.at[n],
                recv_sem=g_r.at[n],
                device_id={"lat": d},
                device_id_type=MESH,
            ).start()

        pltpu.make_async_copy(src(mine), dst.at[xy], g_r.at[n]).start()

    def reduce_1():
        for e in range(XY):
            block, tile = e // 4, e % 4
            cols = pl.ds(128 * tile, 128)
            if block < 2:
                gsnd[e, pl.ds(0, 16), :] = gp[pl.ds(16 * block, 16), cols]
            else:
                gsnd[e, pl.ds(0, 16), :] = ga[pl.ds(16 * (block - 2), 16), cols]
            gsnd[e, pl.ds(16, 1), :] = gp[pl.ds(CH, 1), cols]
        xy_step(0, lambda e: gsnd.at[e], g1, xy)

    def reduce_2():
        pltpu.make_async_copy(g1, g1, g_r.at[0]).wait()
        total = g1[0]
        for e in range(1, XY):
            total = total + g1[e]
        g2s[...] = total
        copy = pltpu.make_async_remote_copy(
            src_ref=g2s,
            dst_ref=g2r,
            send_sem=g_s.at[1],
            recv_sem=g_r.at[1],
            device_id={"lat": me + 1 - 2 * lax.rem(me, 2)},
            device_id_type=MESH,
        )
        copy.start()

    def reduce_3():
        pltpu.make_async_copy(g2r, g2r, g_r.at[1]).wait()
        g3s[...] = g2s[...] + g2r[...]

        @pl.loop(1, GRP)
        def _(k):
            pltpu.make_async_remote_copy(
                src_ref=g3s,
                dst_ref=g3r.at[grp],
                send_sem=g_s.at[2],
                recv_sem=g_r.at[2],
                device_id={"grp": lax.rem(grp + k, GRP)},
                device_id_type=MESH,
            ).start()

        pltpu.make_async_copy(g3s, g3r.at[grp], g_r.at[2]).start()

    def reduce_4():
        pltpu.make_async_copy(g3r, g3r, g_r.at[2]).wait()
        total = g3r[0]
        for e in range(1, GRP):
            total = total + g3r[e]
        g4s[...] = total
        xy_step(3, lambda e: g4s, g4r, xy)

    def reduce_5():
        pltpu.make_async_copy(g4r, g4r, g_r.at[3]).wait()
        gr_ref[...] = g4r[...]

    @pl.loop(0, 4)
    def _(c):
        for now in range(4):

            @pl.when(c == now)
            def _():
                arrive(now)
                if now < 2:
                    forward(now + 4, ready=True)

        racc[...] = jnp.zeros_like(racc)
        lax.fori_loop(0, HALF // JT, physics, 0)
        for now in range(4):

            @pl.when(c == now)
            def _():
                if now == 3:
                    reduce_1()
                turn(now)
                if now > 0:
                    back(now - 1)

    def unpack(n):
        lo, hi = BACK[n]
        span = brcv.at[:, pl.ds(lo, hi - lo)]
        pltpu.make_async_copy(span, span, b_r.at[n]).wait()

        @pl.loop(0, LAT)
        def _(src):
            rf[pl.ds(pl.multiple_of(src * 80 + lo, 8), hi - lo), :] = brcv[
                src, pl.ds(lo, hi - lo), :
            ].astype(F32)

    reduce_2()
    unpack(0)
    reduce_3()
    unpack(1)
    reduce_4()
    unpack(2)

    @pl.loop(0, MB // 4)
    def _(step):
        for sub in range(4):
            mm = 4 * step + sub
            rows = jnp.concatenate(
                [rf[pl.ds(MB * q + mm, LAT, stride=80), :] for q in range(4)], axis=0
            )
            t = rows.T.astype(BF16)
            a_ref[wave(mm)] = jnp.concatenate(
                [
                    jnp.concatenate([t[:32], t[64:96]], axis=0),
                    jnp.concatenate([t[32:64], t[96:]], axis=0),
                ],
                axis=1,
            )

    reduce_5()

    for n, (lo, hi) in enumerate(SEND):
        span = snd.at[pl.ds(0, LAT - 1), pl.ds(lo, hi - lo)]
        pltpu.make_async_copy(span, span, f_s.at[n]).wait()
    for n, (lo, hi) in enumerate(BACK):
        span = bsnd.at[pl.ds(0, LAT - 1), pl.ds(lo, hi - lo)]
        pltpu.make_async_copy(span, span, b_s.at[n]).wait()
    for n, count, buf in ((0, XY - 1, g1), (2, GRP - 1, g3r), (3, XY - 1, g4r)):
        span = buf.at[pl.ds(0, count)]
        pltpu.make_async_copy(span, span, g_s.at[n]).wait()
    pltpu.make_async_copy(g2s, g2s, g_s.at[1]).wait()


def body(
    tables,
    spectral_state, cotangent, legendre, quadrature, damping, physics_in, physics_bias, physics_out,
):
    hbm = pl.BlockSpec(memory_space=pl.ANY)
    vmem = pl.BlockSpec(memory_space=pltpu.VMEM)
    dma = pltpu.SemaphoreType.DMA
    scratch = [
        pltpu.VMEM((MB, 2 * CH, NL), BF16),
        pltpu.VMEM((MB, 2 * CH, NL), BF16),
        pltpu.VMEM((MB, NL, NP), BF16),
        pltpu.VMEM((2, HALF, COLS), BF16),
        pltpu.VMEM((CH, NL), F32),
        pltpu.VMEM((MB * NP, 128), F32),
        pltpu.VMEM((80, 128), F32),
        pltpu.VMEM((LAT, 160, 128), BF16),
        pltpu.VMEM((LAT, 160, 128), BF16),
        pltpu.VMEM((LAT * 80, 128), F32),
        pltpu.VMEM((2, COLS, 128), BF16),
        pltpu.VMEM((2, 256, 2 * HID), BF16),
        pltpu.VMEM((2, 64, COLS), F32),
        pltpu.VMEM((4 * 640, 128), F32),
        pltpu.VMEM((LAT, 80, 128), BF16),
        pltpu.VMEM((LAT, 80, 128), BF16),
        pltpu.VMEM((48, HID), F32),
        pltpu.VMEM((CH, HID), F32),
        pltpu.VMEM((XY, GR, 128), F32),
        pltpu.VMEM((XY, GR, 128), F32),
        pltpu.VMEM((GR, 128), F32),
        pltpu.VMEM((GR, 128), F32),
        pltpu.VMEM((GR, 128), F32),
        pltpu.VMEM((GRP, GR, 128), F32),
        pltpu.VMEM((GR, 128), F32),
        pltpu.VMEM((XY, GR, 128), F32),
        dma((3, MB)),
        dma,
        dma((6,)),
        dma((6,)),
        dma((3,)),
        dma((3,)),
        dma((4,)),
        dma((4,)),
    ]
    fourier, grads = pl.pallas_call(
        kernel,
        out_shape=[
            jax.ShapeDtypeStruct((MB, 2 * CH, NP), BF16),
            jax.ShapeDtypeStruct((XY, GR, 128), F32),
        ],
        in_specs=[hbm] * 4 + [vmem] * 5,
        out_specs=[vmem, vmem],
        scratch_shapes=scratch,
        compiler_params=pltpu.CompilerParams(
            collective_id=0, has_side_effects=True, vmem_limit_bytes=VMEM_LIMIT
        ),
    )(
        spectral_state[0],
        cotangent[0],
        legendre,
        tables,
        quadrature[None, :],
        damping[None, :],
        physics_in.T,
        physics_bias[None, :],
        physics_out,
    )
    whole = lambda *shape: pl.BlockSpec(shape, lambda i: (0,) * len(shape))
    part = lambda *shape: pl.BlockSpec((STEP,) + shape, lambda i: (i, 0, 0))
    grad_state, grad_in, grad_bias, grad_out = pl.pallas_call(
        inverse_kernel,
        grid=(MB // STEP,),
        out_shape=[
            jax.ShapeDtypeStruct((MB, 2 * CH, NL), F32),
            jax.ShapeDtypeStruct((CH, HID), F32),
            jax.ShapeDtypeStruct((1, HID), F32),
            jax.ShapeDtypeStruct((CH, HID), F32),
        ],
        in_specs=[
            part(2 * CH, NP),
            part(2 * CH, NL),
            part(NL, NP),
            whole(1, CH),
            whole(XY, GR, 128),
        ],
        out_specs=[part(2 * CH, NL), whole(CH, HID), whole(1, HID), whole(CH, HID)],
        scratch_shapes=[pltpu.VMEM((2 * CH, NL), F32)],
        compiler_params=pltpu.CompilerParams(vmem_limit_bytes=24 * 2**20),
    )(fourier, cotangent[0], legendre, damping[None, :], grads)
    return (grad_state[None], grad_in.T, grad_bias[0], grad_out)


def solution(mesh):
    in_specs = (
        P(),
        P("grp", "lat", None, None),
        P("grp", "lat", None, None),
        P("lat", None, None),
        P(),
        P(),
        P(),
        P(),
        P(),
    )
    out_specs = (P("grp", "lat", None, None), P(), P(), P())
    mapped = jax.shard_map(body, mesh=mesh, in_specs=in_specs, out_specs=out_specs, check_vma=False)
    tables = longitude_tables()

    def run(*args):
        return mapped(jnp.asarray(tables), *args)

    return run
```

```python
import functools
import math

import jax
import jax.numpy as jnp
import ml_dtypes
import numpy as np
from jax import lax
from jax.experimental import pallas as pl
from jax.experimental.pallas import tpu as pltpu
from jax.sharding import PartitionSpec as P

NLON = 2560
HALF = NLON // 2
MESH = pl.DeviceIdType.MESH
F32, BF16 = jnp.float32, jnp.bfloat16

LAT = 32
GRP = 8
XY = 16
MB = 20
HB = MB // 2
NL = 640
NP = 256
CH = 32
HID = 512
COLS = 640
JT = 640
SEND = ((0, 16), (16, 32), (32, 48), (48, 80), (80, 128), (128, 160))
ARRIVE = ((0, 1, 2), (3,), (4,), (5,))
BACK = ((0, 32), (32, 48), (48, 80))
GR = 17
STEP = 4
VMEM_LIMIT = 54 * 2**20


def table_rows(e):
    if e < 8:
        base = 256 * (e // 4) + LAT * (e % 4)
        return base, base + 128
    return 512 + LAT * (e - 8), 576 + LAT * (e - 8)


def longitude_tables():
    place = np.arange(HALF, dtype=np.int64)[:, None]
    owner = np.arange(LAT, dtype=np.int64)[None, :]
    tables = np.zeros((2, HALF, COLS), np.float64)
    scale = math.sqrt(2.0 / NLON)
    for parity in range(2):
        for e in range(HB):
            wave = MB * owner + 2 * e + parity
            angle = (wave * place % NLON) * (2.0 * math.pi / NLON)
            c, s = table_rows(e)
            tables[parity, :, c : c + LAT] = np.cos(angle) * scale
            tables[parity, :, s : s + LAT] = -np.sin(angle) * scale
    return tables.astype(ml_dtypes.bfloat16)


def dot(a, b, ca, cb):
    return lax.dot_general(a, b, (((ca,), (cb,)), ((), ())), preferred_element_type=F32)


def implicit_factor(damping):
    across = lax.broadcasted_iota(jnp.int32, (CH, CH), 0)
    along = lax.broadcasted_iota(jnp.int32, (CH, CH), 1)
    column = jnp.sum(jnp.where(across == along, damping, 0.0), axis=1, keepdims=True)
    degree = lax.broadcasted_iota(jnp.int32, (CH, NL), 1).astype(F32)
    ratio = degree * (degree + 1.0) / (NL * (NL + 1.0))
    return 1.0 / (1.0 + column * ratio)


def inverse_kernel(a_ref, cot_ref, leg_ref, damp_ref, gr_ref, out_ref, gi_ref, gb_ref, go_ref, fac):
    @pl.when(pl.program_id(0) == 0)
    def _():
        factor = implicit_factor(damp_ref[...])
        fac[...] = jnp.concatenate([factor, factor], axis=0)
        scale = 1.0 / math.sqrt(GRP * NP * NLON)
        for e in range(XY):
            block, tile = e // 4, e % 4
            cols = pl.ds(128 * tile, 128)
            piece = gr_ref[e, pl.ds(0, 16), :] * scale
            if block < 2:
                gi_ref[pl.ds(16 * block, 16), cols] = piece
            else:
                go_ref[pl.ds(16 * (block - 2), 16), cols] = piece
            if block == 0:
                gb_ref[:, cols] = gr_ref[e, pl.ds(16, 1), :] * scale

    for i in range(STEP):
        out_ref[i] = cot_ref[i].astype(F32) * fac[...] + dot(a_ref[i], leg_ref[i], 1, 1)


def kernel(
    spec_hbm, cot_hbm, leg_hbm, tab_hbm, quad_hbm, damp_hbm, pin_hbm, bias_hbm, pout_hbm,
    a_ref, gr_ref,
    quad_ref, damp_ref, pin_ref, bias_ref, pout_ref, spec, cot, leg, tab, factor, ft, stage, snd, rcv, rf, wdft, wp, held, racc, rall, bsnd, brcv,
    gp, ga, gsnd, g1, g2s, g2r, g3s, g3r,
    small_sem, in_sem, tab_sem, f_s, f_r, b_s, b_r, g_s, g_r,
):
    me = lax.axis_index("lat")
    grp = lax.axis_index("grp")
    xy = me // 2
    partner = me + 1 - 2 * lax.rem(me, 2)

    def peer(k):
        return lax.rem(me + k, LAT)

    barrier = pltpu.get_barrier_semaphore()

    @pl.loop(1, LAT)
    def _(k):
        pl.semaphore_signal(barrier, inc=1, device_id={"lat": peer(k)}, device_id_type=MESH)

    @pl.loop(1, GRP)
    def _(k):
        pl.semaphore_signal(
            barrier, inc=1, device_id={"grp": lax.rem(grp + k, GRP)}, device_id_type=MESH
        )

    @pl.loop(1, GRP)
    def _(k):
        pl.semaphore_signal(
            barrier,
            inc=1,
            device_id={"lat": partner, "grp": lax.rem(grp + k, GRP)},
            device_id_type=MESH,
        )

    def wave(mm):
        return 2 * lax.rem(mm, HB) + mm // HB

    def loads(mm):
        m = wave(mm)
        return [
            pltpu.make_async_copy(src.at[m], dst.at[m], in_sem.at[i, mm])
            for i, (src, dst) in enumerate(((spec_hbm, spec), (cot_hbm, cot), (leg_hbm, leg)))
        ]

    small = [
        pltpu.make_async_copy(src, dst, small_sem.at[i])
        for i, (src, dst) in enumerate(
            (
                (damp_hbm, damp_ref),
                (quad_hbm, quad_ref),
                (pin_hbm, pin_ref),
                (bias_hbm, bias_ref),
                (pout_hbm, pout_ref),
            )
        )
    ]
    for copy in small:
        copy.start()

    @pl.loop(0, MB)
    def _(mm):
        for copy in loads(mm):
            copy.start()

    tab_copy = pltpu.make_async_copy(tab_hbm, tab, tab_sem)
    tab_copy.start()

    for copy in small:
        copy.wait()
    factor[...] = implicit_factor(damp_ref[...])

    def legendre(mm):
        m = wave(mm)
        for copy in loads(mm):
            copy.wait()
        fac = factor[...]
        s = spec[m]
        c = cot[m].astype(F32)
        c_re = (c[:CH] * fac).astype(BF16)
        c_im = (c[CH:] * fac).astype(BF16)
        lhs = jnp.concatenate([s[:CH], c_re, s[CH:], c_im], axis=0)
        four = dot(lhs, leg[m], 1, 0)
        quad = quad_ref[...]
        four = jnp.concatenate(
            [four[:32], four[32:64] * quad, four[64:96], four[96:] * quad], axis=0
        )
        ft[pl.ds(pl.multiple_of(mm * NP, NP), NP), :] = four.T

    def tile(q, t, d):
        rows = [
            ft[pl.ds(8 * t * NP + 128 * half + 32 * q + d, 8, stride=NP), :] for half in range(2)
        ]
        return jnp.concatenate(rows, axis=0).astype(BF16)

    def rest(pair, d):
        for j in range(4):
            row = 16 * NP + 128 * (j % 2) + 32 * (2 * pair + j // 2) + d
            stage[pl.ds(4 * j, 4), :] = ft[pl.ds(row, 4, stride=NP), :]
        return stage[pl.ds(0, 16), :].astype(BF16)

    def assemble(n, d):
        if n < 2:
            snd[d, pl.ds(16 * n, 16), :] = tile(0, n, d)
        elif n == 2:
            snd[d, pl.ds(32, 16), :] = rest(0, d)
        elif n == 3:
            for t in range(2):
                snd[d, pl.ds(48 + 16 * t, 16), :] = tile(1, t, d)
        elif n == 4:
            for t in range(2):
                snd[d, pl.ds(80 + 16 * t, 16), :] = tile(2, t, d)
            snd[d, pl.ds(112, 16), :] = rest(1, d)
        else:
            for t in range(2):
                snd[d, pl.ds(128 + 16 * t, 16), :] = tile(3, t, d)

    def send(n, d):
        lo, hi = SEND[n]
        pltpu.make_async_remote_copy(
            src_ref=snd.at[d, pl.ds(lo, hi - lo)],
            dst_ref=rcv.at[me, pl.ds(lo, hi - lo)],
            send_sem=f_s.at[n],
            recv_sem=f_r.at[n],
            device_id={"lat": d},
            device_id_type=MESH,
        ).start()

    def far_then_near(f):
        @pl.loop(0, LAT // 2)
        def _(i):
            f(peer(2 * i + 1))

        @pl.loop(1, LAT // 2)
        def _(i):
            f(peer(2 * i))

    def forward(n, ready=False):
        def f(d):
            if not ready:
                assemble(n, d)
            send(n, d)

        far_then_near(f)
        if not ready:
            assemble(n, me)
        lo, hi = SEND[n]
        pltpu.make_async_copy(
            snd.at[me, pl.ds(lo, hi - lo)], rcv.at[me, pl.ds(lo, hi - lo)], f_r.at[n]
        ).start()

    pl.loop(0, 8)(legendre)
    pl.semaphore_wait(barrier, LAT - 1 + 2 * (GRP - 1))
    forward(0)
    pl.loop(8, 16)(legendre)
    forward(1)
    pl.loop(16, MB)(legendre)
    forward(2)
    forward(3)

    @pl.loop(0, LAT)
    def _(d):
        assemble(4, d)
        assemble(5, d)

    wp[...] = jnp.zeros_like(wp)
    half_in = (0.5 * pin_ref[...].astype(F32)).astype(BF16)
    half_out = (0.5 * pout_ref[...].astype(F32)).astype(BF16)
    half_bias = 0.5 * bias_ref[...]
    top = half_bias.astype(BF16).astype(F32)
    mid = (half_bias - top).astype(BF16).astype(F32)
    low = half_bias - top - mid
    row = lax.broadcasted_iota(jnp.int32, (16, HID), 0)
    bias_rows = jnp.where(
        row == 0, top, jnp.where(row == 1, mid, jnp.where(row == 2, low, 0.0))
    ).astype(BF16)
    for s in range(2):
        wp[s, pl.ds(64 * s, CH), pl.ds(0, HID)] = half_in
        wp[s, pl.ds(64 * s + CH, CH), pl.ds(HID, HID)] = half_out
        wp[s, pl.ds(128, 16), pl.ds(0, HID)] = bias_rows
    gp[...] = jnp.zeros_like(gp)
    ga[...] = jnp.zeros_like(ga)
    tab_copy.wait()

    lane = lax.broadcasted_iota(jnp.int32, (LAT, 128), 1)
    left = lane < 64

    def arrive(c):
        for n in ARRIVE[c]:
            lo, hi = SEND[n]
            span = rcv.at[:, pl.ds(lo, hi - lo)]
            pltpu.make_async_copy(span, span, f_r.at[n]).wait()
            at = lo % 80

            @pl.loop(0, LAT)
            def _(src):
                rf[pl.ds(pl.multiple_of(src * 80 + at, 8), hi - lo), :] = rcv[
                    src, pl.ds(lo, hi - lo), :
                ].astype(F32)

        def row(half, mm):
            if mm < 16:
                return 48 * (c % 2) + 16 * (mm // 8) + 8 * half + mm % 8
            return 32 + 8 * (c % 2) + 4 * half + mm - 16

        for mm in range(MB):
            w0 = rf[pl.ds(row(0, mm), LAT, stride=80), :]
            w1 = rf[pl.ds(row(1, mm), LAT, stride=80), :]
            re = jnp.where(left, w0, pltpu.roll(w1, 64, 1))
            im = jnp.where(left, pltpu.roll(w0, 64, 1), w1)
            r_re, r_im = table_rows(mm % HB)
            wdft[mm // HB, pl.ds(r_re, LAT), :] = re.astype(BF16)
            wdft[mm // HB, pl.ds(r_im, LAT), :] = im.astype(BF16)

    one_lane = lax.broadcasted_iota(jnp.int32, (2 * JT, 128), 1)
    ones = jnp.where(one_lane < 3, 1.0, 0.0).astype(BF16)
    ones_t = jnp.ones((16, 2 * JT), BF16)

    def columns(i, grid_gradient):
        span = pl.ds(pl.multiple_of(i * JT, JT), JT)
        even = dot(tab[0, span, :], wdft[0], 1, 0)
        odd = dot(tab[1, span, :], wdft[1], 1, 0)
        x = jnp.concatenate([(even + odd).astype(BF16), (even - odd).astype(BF16)], axis=0)
        xe = jnp.concatenate([x, ones], axis=1)
        xt = x.T
        grads = []
        for s in range(2):
            h = dot(xe, wp[s, :, pl.ds(0, HID)], 1, 0)
            u = dot(xe, wp[s, :, pl.ds(HID, HID)], 1, 0)
            a = 1.0 + jnp.tanh(h)
            act = h * a
            pre = (u * (a * ((1.0 + (h + h)) - act))).astype(BF16)
            act = act.astype(BF16)
            grads.append(grid_gradient(s, pre))
            lhs = jnp.concatenate([xt[64 * s : 64 * s + CH], ones_t], axis=0)
            gp[...] += dot(lhs, pre, 1, 0)
            ga[...] += dot(xt[64 * s + CH : 64 * s + 64], act, 1, 0)
        return grads

    def longitudes(i, grads):
        span = pl.ds(pl.multiple_of(i * JT, JT), JT)
        gg = jnp.concatenate(grads, axis=0)
        g_even = (gg[:, :JT] + gg[:, JT:]).astype(BF16)
        g_odd = (gg[:, :JT] - gg[:, JT:]).astype(BF16)
        racc[0] += dot(g_even, tab[0, span, :], 1, 0)
        racc[1] += dot(g_odd, tab[1, span, :], 1, 0)

    def physics(i):
        longitudes(i, columns(i, lambda s, pre: dot(pin_ref[...], pre, 1, 1)))

    def hold(i):
        def keep(s, pre):
            held[i, s] = pre

        columns(i, keep)

    def finish(i):
        longitudes(i, [dot(pin_ref[...], held[i, s], 1, 1) for s in range(2)])

    def turn(c):
        for parity in range(2):
            r = racc[parity]
            base = 640 * c + 320 * parity
            rall[pl.ds(base, 128), :] = jnp.concatenate([r[:, :128], r[:, 128:256]], axis=0).T
            rall[pl.ds(base + 128, 128), :] = jnp.concatenate(
                [r[:, 256:384], r[:, 384:512]], axis=0
            ).T
            last = r[:, 512:]
            both = jnp.concatenate([last, pltpu.roll(last, 64, 1)], axis=0).T
            rall[pl.ds(base + 256, 64), :] = both[:64]

    def pack(n, d):
        lo, hi = BACK[n]
        for q in range(lo // MB, (hi - 1) // MB + 1):
            stage[pl.ds(MB * q, MB), :] = rall[pl.ds(640 * q + d, MB, stride=LAT), :]
        bsnd[d, pl.ds(lo, hi - lo), :] = stage[pl.ds(lo, hi - lo), :].astype(BF16)

    def back(n, ready=False):
        lo, hi = BACK[n]

        def go(d):
            if not ready:
                pack(n, d)
            pltpu.make_async_remote_copy(
                src_ref=bsnd.at[d, pl.ds(lo, hi - lo)],
                dst_ref=brcv.at[me, pl.ds(lo, hi - lo)],
                send_sem=b_s.at[n],
                recv_sem=b_r.at[n],
                device_id={"lat": d},
                device_id_type=MESH,
            ).start()

        far_then_near(go)
        if not ready:
            pack(n, me)
        pltpu.make_async_copy(
            bsnd.at[me, pl.ds(lo, hi - lo)], brcv.at[me, pl.ds(lo, hi - lo)], b_r.at[n]
        ).start()

    def xy_step(n, src, dst, mine):
        @pl.loop(1, XY)
        def _(i):
            d = peer(2 * i)
            pltpu.make_async_remote_copy(
                src_ref=src(d // 2),
                dst_ref=dst.at[xy],
                send_sem=g_s.at[n],
                recv_sem=g_r.at[n],
                device_id={"lat": d},
                device_id_type=MESH,
            ).start()

        pltpu.make_async_copy(src(mine), dst.at[xy], g_r.at[n]).start()

    def reduce_1():
        for e in range(XY):
            block, tile = e // 4, e % 4
            cols = pl.ds(128 * tile, 128)
            if block < 2:
                gsnd[e, pl.ds(0, 16), :] = gp[pl.ds(16 * block, 16), cols]
            else:
                gsnd[e, pl.ds(0, 16), :] = ga[pl.ds(16 * (block - 2), 16), cols]
            gsnd[e, pl.ds(16, 1), :] = gp[pl.ds(CH, 1), cols]
        xy_step(0, lambda e: gsnd.at[e], g1, xy)

    def reduce_2():
        pltpu.make_async_copy(g1, g1, g_r.at[0]).wait()
        total = g1[0]
        for e in range(1, XY):
            total = total + g1[e]
        g2s[...] = total

        for far in (1, 0):

            @pl.loop(1 - far, GRP)
            def _(k):
                pltpu.make_async_remote_copy(
                    src_ref=g2s,
                    dst_ref=g2r.at[GRP * lax.rem(me, 2) + grp],
                    send_sem=g_s.at[1],
                    recv_sem=g_r.at[1],
                    device_id={
                        "lat": partner if far else me,
                        "grp": lax.rem(grp + k, GRP),
                    },
                    device_id_type=MESH,
                ).start()

        pltpu.make_async_copy(g2s, g2r.at[GRP * lax.rem(me, 2) + grp], g_r.at[1]).start()

    def reduce_3():
        pltpu.make_async_copy(g2r, g2r, g_r.at[1]).wait()
        total = g2r[0]
        for e in range(1, 2 * GRP):
            total = total + g2r[e]
        g3s[...] = total
        xy_step(2, lambda e: g3s, g3r, xy)

    def reduce_4():
        pltpu.make_async_copy(g3r, g3r, g_r.at[2]).wait()
        gr_ref[...] = g3r[...]

    @pl.loop(0, 4)
    def _(c):
        for now in range(4):

            @pl.when(c == now)
            def _():
                arrive(now)
                if now < 2:
                    forward(now + 4, ready=True)

        racc[...] = jnp.zeros_like(racc)

        @pl.when(c < 3)
        def _():
            pl.loop(0, HALF // JT)(physics)

        @pl.when(c == 3)
        def _():
            pl.loop(0, HALF // JT)(hold)
            reduce_1()
            pl.loop(0, HALF // JT)(finish)

        for now in range(4):

            @pl.when(c == now)
            def _():
                turn(now)
                if now in (1, 2):
                    back(now - 1)

    @pl.loop(0, LAT)
    def _(d):
        pack(2, d)

    reduce_2()
    back(2, ready=True)

    def unpack(n):
        lo, hi = BACK[n]
        span = brcv.at[:, pl.ds(lo, hi - lo)]
        pltpu.make_async_copy(span, span, b_r.at[n]).wait()

        @pl.loop(0, LAT)
        def _(src):
            rf[pl.ds(pl.multiple_of(src * 80 + lo, 8), hi - lo), :] = brcv[
                src, pl.ds(lo, hi - lo), :
            ].astype(F32)

    unpack(0)
    unpack(1)
    reduce_3()
    unpack(2)

    @pl.loop(0, MB // 4)
    def _(step):
        for sub in range(4):
            mm = 4 * step + sub
            rows = jnp.concatenate(
                [rf[pl.ds(MB * q + mm, LAT, stride=80), :] for q in range(4)], axis=0
            )
            t = rows.T.astype(BF16)
            a_ref[wave(mm)] = jnp.concatenate(
                [
                    jnp.concatenate([t[:32], t[64:96]], axis=0),
                    jnp.concatenate([t[32:64], t[96:]], axis=0),
                ],
                axis=1,
            )

    reduce_4()

    for n, (lo, hi) in enumerate(SEND):
        span = snd.at[pl.ds(0, LAT - 1), pl.ds(lo, hi - lo)]
        pltpu.make_async_copy(span, span, f_s.at[n]).wait()
    for n, (lo, hi) in enumerate(BACK):
        span = bsnd.at[pl.ds(0, LAT - 1), pl.ds(lo, hi - lo)]
        pltpu.make_async_copy(span, span, b_s.at[n]).wait()
    for n, count, buf in ((0, XY - 1, g1), (1, 2 * GRP - 1, g2r), (2, XY - 1, g3r)):
        span = buf.at[pl.ds(0, count)]
        pltpu.make_async_copy(span, span, g_s.at[n]).wait()


def body(
    tables,
    spectral_state, cotangent, legendre, quadrature, damping, physics_in, physics_bias, physics_out,
):
    hbm = pl.BlockSpec(memory_space=pl.ANY)
    vmem = pl.BlockSpec(memory_space=pltpu.VMEM)
    dma = pltpu.SemaphoreType.DMA
    scratch = [
        pltpu.VMEM((1, NP), F32),
        pltpu.VMEM((1, CH), F32),
        pltpu.VMEM((CH, HID), BF16),
        pltpu.VMEM((1, HID), F32),
        pltpu.VMEM((CH, HID), BF16),
        pltpu.VMEM((MB, 2 * CH, NL), BF16),
        pltpu.VMEM((MB, 2 * CH, NL), BF16),
        pltpu.VMEM((MB, NL, NP), BF16),
        pltpu.VMEM((2, HALF, COLS), BF16),
        pltpu.VMEM((CH, NL), F32),
        pltpu.VMEM((MB * NP, 128), F32),
        pltpu.VMEM((80, 128), F32),
        pltpu.VMEM((LAT, 160, 128), BF16),
        pltpu.VMEM((LAT, 160, 128), BF16),
        pltpu.VMEM((LAT * 80, 128), F32),
        pltpu.VMEM((2, COLS, 128), BF16),
        pltpu.VMEM((2, 256, 2 * HID), BF16),
        pltpu.VMEM((HALF // JT, 2, 2 * JT, HID), BF16),
        pltpu.VMEM((2, 64, COLS), F32),
        pltpu.VMEM((4 * 640, 128), F32),
        pltpu.VMEM((LAT, 80, 128), BF16),
        pltpu.VMEM((LAT, 80, 128), BF16),
        pltpu.VMEM((48, HID), F32),
        pltpu.VMEM((CH, HID), F32),
        pltpu.VMEM((XY, GR, 128), F32),
        pltpu.VMEM((XY, GR, 128), F32),
        pltpu.VMEM((GR, 128), F32),
        pltpu.VMEM((2 * GRP, GR, 128), F32),
        pltpu.VMEM((GR, 128), F32),
        pltpu.VMEM((XY, GR, 128), F32),
        dma((5,)),
        dma((3, MB)),
        dma,
        dma((6,)),
        dma((6,)),
        dma((3,)),
        dma((3,)),
        dma((3,)),
        dma((3,)),
    ]
    fourier, grads = pl.pallas_call(
        kernel,
        out_shape=[
            jax.ShapeDtypeStruct((MB, 2 * CH, NP), BF16),
            jax.ShapeDtypeStruct((XY, GR, 128), F32),
        ],
        in_specs=[hbm] * 9,
        out_specs=[vmem, vmem],
        scratch_shapes=scratch,
        compiler_params=pltpu.CompilerParams(
            collective_id=0, has_side_effects=True, vmem_limit_bytes=VMEM_LIMIT
        ),
    )(
        spectral_state[0],
        cotangent[0],
        legendre,
        tables,
        quadrature[None, :],
        damping[None, :],
        physics_in.T,
        physics_bias[None, :],
        physics_out,
    )
    whole = lambda *shape: pl.BlockSpec(shape, lambda i: (0,) * len(shape))
    part = lambda *shape: pl.BlockSpec((STEP,) + shape, lambda i: (i, 0, 0))
    grad_state, grad_in, grad_bias, grad_out = pl.pallas_call(
        inverse_kernel,
        grid=(MB // STEP,),
        out_shape=[
            jax.ShapeDtypeStruct((MB, 2 * CH, NL), F32),
            jax.ShapeDtypeStruct((CH, HID), F32),
            jax.ShapeDtypeStruct((1, HID), F32),
            jax.ShapeDtypeStruct((CH, HID), F32),
        ],
        in_specs=[
            part(2 * CH, NP),
            part(2 * CH, NL),
            part(NL, NP),
            whole(1, CH),
            whole(XY, GR, 128),
        ],
        out_specs=[part(2 * CH, NL), whole(CH, HID), whole(1, HID), whole(CH, HID)],
        scratch_shapes=[pltpu.VMEM((2 * CH, NL), F32)],
        compiler_params=pltpu.CompilerParams(vmem_limit_bytes=24 * 2**20),
    )(fourier, cotangent[0], legendre, damping[None, :], grads)
    return (grad_state[None], grad_in.T, grad_bias[0], grad_out)


def solution(mesh):
    in_specs = (
        P(),
        P("grp", "lat", None, None),
        P("grp", "lat", None, None),
        P("lat", None, None),
        P(),
        P(),
        P(),
        P(),
        P(),
    )
    out_specs = (P("grp", "lat", None, None), P(), P(), P())
    mapped = jax.shard_map(body, mesh=mesh, in_specs=in_specs, out_specs=out_specs, check_vma=False)
    tables = longitude_tables()

    def run(*args):
        return mapped(jnp.asarray(tables), *args)

    return run
```

```python
import functools
import math

import jax
import jax.numpy as jnp
import ml_dtypes
import numpy as np
from jax import lax
from jax.experimental import pallas as pl
from jax.experimental.pallas import tpu as pltpu
from jax.sharding import PartitionSpec as P

NLON = 2560
HALF = NLON // 2
MESH = pl.DeviceIdType.MESH
F32, BF16 = jnp.float32, jnp.bfloat16

LAT = 32
GRP = 8
XY = 16
MB = 20
HB = MB // 2
NL = 640
NP = 256
CH = 32
HID = 512
COLS = 640
JT = 640
SEND = ((0, 16), (16, 32), (32, 48), (48, 80), (80, 128), (128, 160))
ARRIVE = ((0, 1, 2), (3,), (4,), (5,))
BACK = ((0, 32), (32, 48), (48, 80))
GR = 17
STEP = 10
VMEM_LIMIT = 54 * 2**20


def table_rows(e):
    if e < 8:
        base = 256 * (e // 4) + LAT * (e % 4)
        return base, base + 128
    return 512 + LAT * (e - 8), 576 + LAT * (e - 8)


def longitude_tables():
    place = np.arange(HALF, dtype=np.int64)[:, None]
    owner = np.arange(LAT, dtype=np.int64)[None, :]
    tables = np.zeros((2, HALF, COLS), np.float64)
    scale = math.sqrt(2.0 / NLON)
    for parity in range(2):
        for e in range(HB):
            wave = MB * owner + 2 * e + parity
            angle = (wave * place % NLON) * (2.0 * math.pi / NLON)
            c, s = table_rows(e)
            tables[parity, :, c : c + LAT] = np.cos(angle) * scale
            tables[parity, :, s : s + LAT] = -np.sin(angle) * scale
    return tables.astype(ml_dtypes.bfloat16)


def dot(a, b, ca, cb):
    return lax.dot_general(a, b, (((ca,), (cb,)), ((), ())), preferred_element_type=F32)


def implicit_factor(damping):
    across = lax.broadcasted_iota(jnp.int32, (CH, CH), 0)
    along = lax.broadcasted_iota(jnp.int32, (CH, CH), 1)
    column = jnp.sum(jnp.where(across == along, damping, 0.0), axis=1, keepdims=True)
    degree = lax.broadcasted_iota(jnp.int32, (CH, NL), 1).astype(F32)
    ratio = degree * (degree + 1.0) / (NL * (NL + 1.0))
    return 1.0 / (1.0 + column * ratio)


def inverse_kernel(a_ref, cot_ref, leg_ref, damp_ref, gr_ref, out_ref, gi_ref, gb_ref, go_ref, fac):
    @pl.when(pl.program_id(0) == 0)
    def _():
        factor = implicit_factor(damp_ref[...])
        fac[...] = jnp.concatenate([factor, factor], axis=0)
        scale = 1.0 / math.sqrt(GRP * NP * NLON)
        for e in range(XY):
            block, tile = e // 4, e % 4
            cols = pl.ds(128 * tile, 128)
            piece = gr_ref[e, pl.ds(0, 16), :] * scale
            if block < 2:
                gi_ref[pl.ds(16 * block, 16), cols] = piece
            else:
                go_ref[pl.ds(16 * (block - 2), 16), cols] = piece
            if block == 0:
                gb_ref[:, cols] = gr_ref[e, pl.ds(16, 1), :] * scale

    for i in range(STEP):
        out_ref[i] = cot_ref[i].astype(F32) * fac[...] + dot(a_ref[i], leg_ref[i], 1, 1)


def kernel(
    spec_hbm, cot_hbm, leg_hbm, tab_hbm, quad_hbm, damp_hbm, pin_hbm, bias_hbm, pout_hbm,
    a_ref, gr_ref,
    quad_ref, damp_ref, pin_ref, bias_ref, pout_ref, spec, cot, leg, tab, factor, ft, stage, snd, rcv, rf, wdft, wp, held, racc, rall, bsnd, brcv,
    gp, ga, gsnd, g1, g2s, g2r, g3s, g3r,
    small_sem, in_sem, tab_sem, f_s, f_r, b_s, b_r, g_s, g_r,
):
    me = lax.axis_index("lat")
    grp = lax.axis_index("grp")
    xy = me // 2
    partner = me + 1 - 2 * lax.rem(me, 2)

    def peer(k):
        return lax.rem(me + k, LAT)

    barrier = pltpu.get_barrier_semaphore()

    @pl.loop(1, LAT)
    def _(k):
        pl.semaphore_signal(barrier, inc=1, device_id={"lat": peer(k)}, device_id_type=MESH)

    @pl.loop(1, GRP)
    def _(k):
        pl.semaphore_signal(
            barrier, inc=1, device_id={"grp": lax.rem(grp + k, GRP)}, device_id_type=MESH
        )

    @pl.loop(1, GRP)
    def _(k):
        pl.semaphore_signal(
            barrier,
            inc=1,
            device_id={"lat": partner, "grp": lax.rem(grp + k, GRP)},
            device_id_type=MESH,
        )

    def wave(mm):
        return 2 * lax.rem(mm, HB) + mm // HB

    def loads(mm):
        m = wave(mm)
        return [
            pltpu.make_async_copy(src.at[m], dst.at[m], in_sem.at[i, mm])
            for i, (src, dst) in enumerate(((spec_hbm, spec), (cot_hbm, cot), (leg_hbm, leg)))
        ]

    small = [
        pltpu.make_async_copy(src, dst, small_sem.at[i])
        for i, (src, dst) in enumerate(
            (
                (damp_hbm, damp_ref),
                (quad_hbm, quad_ref),
                (pin_hbm, pin_ref),
                (bias_hbm, bias_ref),
                (pout_hbm, pout_ref),
            )
        )
    ]
    for copy in small:
        copy.start()

    @pl.loop(0, MB)
    def _(mm):
        for copy in loads(mm):
            copy.start()

    tab_copy = pltpu.make_async_copy(tab_hbm, tab, tab_sem)

    for copy in small:
        copy.wait()
    factor[...] = implicit_factor(damp_ref[...])

    def legendre(mm):
        m = wave(mm)
        for copy in loads(mm):
            copy.wait()
        fac = factor[...]
        s = spec[m]
        c = cot[m].astype(F32)
        c_re = (c[:CH] * fac).astype(BF16)
        c_im = (c[CH:] * fac).astype(BF16)
        lhs = jnp.concatenate([s[:CH], c_re, s[CH:], c_im], axis=0)
        four = dot(lhs, leg[m], 1, 0)
        quad = quad_ref[...]
        four = jnp.concatenate(
            [four[:32], four[32:64] * quad, four[64:96], four[96:] * quad], axis=0
        )
        ft[pl.ds(pl.multiple_of(mm * NP, NP), NP), :] = four.T

    def tile(q, t, d):
        rows = [
            ft[pl.ds(8 * t * NP + 128 * half + 32 * q + d, 8, stride=NP), :] for half in range(2)
        ]
        return jnp.concatenate(rows, axis=0).astype(BF16)

    def rest(pair, d):
        for j in range(4):
            row = 16 * NP + 128 * (j % 2) + 32 * (2 * pair + j // 2) + d
            stage[pl.ds(4 * j, 4), :] = ft[pl.ds(row, 4, stride=NP), :]
        return stage[pl.ds(0, 16), :].astype(BF16)

    def assemble(n, d):
        if n < 2:
            snd[d, pl.ds(16 * n, 16), :] = tile(0, n, d)
        elif n == 2:
            snd[d, pl.ds(32, 16), :] = rest(0, d)
        elif n == 3:
            for t in range(2):
                snd[d, pl.ds(48 + 16 * t, 16), :] = tile(1, t, d)
        elif n == 4:
            for t in range(2):
                snd[d, pl.ds(80 + 16 * t, 16), :] = tile(2, t, d)
            snd[d, pl.ds(112, 16), :] = rest(1, d)
        else:
            for t in range(2):
                snd[d, pl.ds(128 + 16 * t, 16), :] = tile(3, t, d)

    def send(n, d):
        lo, hi = SEND[n]
        pltpu.make_async_remote_copy(
            src_ref=snd.at[d, pl.ds(lo, hi - lo)],
            dst_ref=rcv.at[me, pl.ds(lo, hi - lo)],
            send_sem=f_s.at[n],
            recv_sem=f_r.at[n],
            device_id={"lat": d},
            device_id_type=MESH,
        ).start()

    def far(f):
        @pl.loop(0, LAT // 2)
        def _(i):
            f(peer(2 * i + 1))

    def near(f):
        @pl.loop(1, LAT // 2)
        def _(i):
            f(peer(2 * i))

    def far_then_near(f):
        far(f)
        near(f)

    def forward(n, ready=False):
        def f(d):
            if not ready:
                assemble(n, d)
            send(n, d)

        far_then_near(f)
        if not ready:
            assemble(n, me)
        lo, hi = SEND[n]
        pltpu.make_async_copy(
            snd.at[me, pl.ds(lo, hi - lo)], rcv.at[me, pl.ds(lo, hi - lo)], f_r.at[n]
        ).start()

    pl.loop(0, 8)(legendre)
    pl.semaphore_wait(barrier, LAT - 1 + 2 * (GRP - 1))
    forward(0)
    pl.loop(8, 16)(legendre)
    forward(1)
    pl.loop(16, MB)(legendre)
    tab_copy.start()
    forward(2)
    forward(3)
    forward(4)

    @pl.loop(0, LAT)
    def _(d):
        assemble(5, d)

    wp[...] = jnp.zeros_like(wp)
    half_in = (0.5 * pin_ref[...].astype(F32)).astype(BF16)
    half_out = (0.5 * pout_ref[...].astype(F32)).astype(BF16)
    half_bias = 0.5 * bias_ref[...]
    top = half_bias.astype(BF16).astype(F32)
    mid = (half_bias - top).astype(BF16).astype(F32)
    low = half_bias - top - mid
    row = lax.broadcasted_iota(jnp.int32, (16, HID), 0)
    bias_rows = jnp.where(
        row == 0, top, jnp.where(row == 1, mid, jnp.where(row == 2, low, 0.0))
    ).astype(BF16)
    for s in range(2):
        wp[s, pl.ds(64 * s, CH), pl.ds(0, HID)] = half_in
        wp[s, pl.ds(64 * s + CH, CH), pl.ds(HID, HID)] = half_out
        wp[s, pl.ds(128, 16), pl.ds(0, HID)] = bias_rows
    gp[...] = jnp.zeros_like(gp)
    ga[...] = jnp.zeros_like(ga)
    tab_copy.wait()

    lane = lax.broadcasted_iota(jnp.int32, (LAT, 128), 1)
    left = lane < 64

    def arrive(c):
        for n in ARRIVE[c]:
            lo, hi = SEND[n]
            span = rcv.at[:, pl.ds(lo, hi - lo)]
            pltpu.make_async_copy(span, span, f_r.at[n]).wait()
            at = lo % 80

            @pl.loop(0, LAT)
            def _(src):
                rf[pl.ds(pl.multiple_of(src * 80 + at, 8), hi - lo), :] = rcv[
                    src, pl.ds(lo, hi - lo), :
                ].astype(F32)

        def row(half, mm):
            if mm < 16:
                return 48 * (c % 2) + 16 * (mm // 8) + 8 * half + mm % 8
            return 32 + 8 * (c % 2) + 4 * half + mm - 16

        for mm in range(MB):
            w0 = rf[pl.ds(row(0, mm), LAT, stride=80), :]
            w1 = rf[pl.ds(row(1, mm), LAT, stride=80), :]
            re = jnp.where(left, w0, pltpu.roll(w1, 64, 1))
            im = jnp.where(left, pltpu.roll(w0, 64, 1), w1)
            r_re, r_im = table_rows(mm % HB)
            wdft[mm // HB, pl.ds(r_re, LAT), :] = re.astype(BF16)
            wdft[mm // HB, pl.ds(r_im, LAT), :] = im.astype(BF16)

    one_lane = lax.broadcasted_iota(jnp.int32, (2 * JT, 128), 1)
    ones = jnp.where(one_lane < 3, 1.0, 0.0).astype(BF16)
    ones_t = jnp.ones((16, 2 * JT), BF16)

    def columns(i, grid_gradient):
        span = pl.ds(pl.multiple_of(i * JT, JT), JT)
        even = dot(tab[0, span, :], wdft[0], 1, 0)
        odd = dot(tab[1, span, :], wdft[1], 1, 0)
        x = jnp.concatenate([(even + odd).astype(BF16), (even - odd).astype(BF16)], axis=0)
        xe = jnp.concatenate([x, ones], axis=1)
        xt = x.T
        grads = []
        for s in range(2):
            h = dot(xe, wp[s, :, pl.ds(0, HID)], 1, 0)
            u = dot(xe, wp[s, :, pl.ds(HID, HID)], 1, 0)
            a = 1.0 + jnp.tanh(h)
            act = h * a
            pre = (u * (a * ((1.0 + (h + h)) - act))).astype(BF16)
            act = act.astype(BF16)
            grads.append(grid_gradient(s, pre))
            lhs = jnp.concatenate([xt[64 * s : 64 * s + CH], ones_t], axis=0)
            gp[...] += dot(lhs, pre, 1, 0)
            ga[...] += dot(xt[64 * s + CH : 64 * s + 64], act, 1, 0)
        return grads

    def longitudes(i, grads):
        span = pl.ds(pl.multiple_of(i * JT, JT), JT)
        gg = jnp.concatenate(grads, axis=0)
        g_even = (gg[:, :JT] + gg[:, JT:]).astype(BF16)
        g_odd = (gg[:, :JT] - gg[:, JT:]).astype(BF16)
        racc[0] += dot(g_even, tab[0, span, :], 1, 0)
        racc[1] += dot(g_odd, tab[1, span, :], 1, 0)

    def physics(i):
        longitudes(i, columns(i, lambda s, pre: dot(pin_ref[...], pre, 1, 1)))

    def hold(i):
        def keep(s, pre):
            held[i, s] = pre

        columns(i, keep)

    def finish(i):
        longitudes(i, [dot(pin_ref[...], held[i, s], 1, 1) for s in range(2)])

    def turn(c):
        for parity in range(2):
            r = racc[parity]
            base = 640 * c + 320 * parity
            rall[pl.ds(base, 128), :] = jnp.concatenate([r[:, :128], r[:, 128:256]], axis=0).T
            rall[pl.ds(base + 128, 128), :] = jnp.concatenate(
                [r[:, 256:384], r[:, 384:512]], axis=0
            ).T
            last = r[:, 512:]
            both = jnp.concatenate([last, pltpu.roll(last, 64, 1)], axis=0).T
            rall[pl.ds(base + 256, 64), :] = both[:64]

    def pack(n, d):
        lo, hi = BACK[n]
        for q in range(lo // MB, (hi - 1) // MB + 1):
            stage[pl.ds(MB * q, MB), :] = rall[pl.ds(640 * q + d, MB, stride=LAT), :]
        bsnd[d, pl.ds(lo, hi - lo), :] = stage[pl.ds(lo, hi - lo), :].astype(BF16)

    def back(n):
        lo, hi = BACK[n]

        def go(d):
            pack(n, d)
            go_packed(d)

        def go_packed(d):
            pltpu.make_async_remote_copy(
                src_ref=bsnd.at[d, pl.ds(lo, hi - lo)],
                dst_ref=brcv.at[me, pl.ds(lo, hi - lo)],
                send_sem=b_s.at[n],
                recv_sem=b_r.at[n],
                device_id={"lat": d},
                device_id_type=MESH,
            ).start()

        if n < 2:
            far_then_near(go)
        else:
            near(go)
        pack(n, me)
        pltpu.make_async_copy(
            bsnd.at[me, pl.ds(lo, hi - lo)], brcv.at[me, pl.ds(lo, hi - lo)], b_r.at[n]
        ).start()
        if n == 2:
            pl.loop(0, LAT // 2)(lambda i: pack(n, peer(2 * i + 1)))
            reduce_2()
            far(go_packed)

    def xy_step(n, src, dst, mine):
        @pl.loop(1, XY)
        def _(i):
            d = peer(2 * i)
            pltpu.make_async_remote_copy(
                src_ref=src(d // 2),
                dst_ref=dst.at[xy],
                send_sem=g_s.at[n],
                recv_sem=g_r.at[n],
                device_id={"lat": d},
                device_id_type=MESH,
            ).start()

        pltpu.make_async_copy(src(mine), dst.at[xy], g_r.at[n]).start()

    def reduce_1():
        for e in range(XY):
            block, tile = e // 4, e % 4
            cols = pl.ds(128 * tile, 128)
            if block < 2:
                gsnd[e, pl.ds(0, 16), :] = gp[pl.ds(16 * block, 16), cols]
            else:
                gsnd[e, pl.ds(0, 16), :] = ga[pl.ds(16 * (block - 2), 16), cols]
            gsnd[e, pl.ds(16, 1), :] = gp[pl.ds(CH, 1), cols]
        xy_step(0, lambda e: gsnd.at[e], g1, xy)

    def reduce_2():
        pltpu.make_async_copy(g1, g1, g_r.at[0]).wait()
        total = g1[0]
        for e in range(1, XY):
            total = total + g1[e]
        g2s[...] = total

        for far in (1, 0):

            @pl.loop(1 - far, GRP)
            def _(k):
                pltpu.make_async_remote_copy(
                    src_ref=g2s,
                    dst_ref=g2r.at[GRP * lax.rem(me, 2) + grp],
                    send_sem=g_s.at[1],
                    recv_sem=g_r.at[1],
                    device_id={
                        "lat": partner if far else me,
                        "grp": lax.rem(grp + k, GRP),
                    },
                    device_id_type=MESH,
                ).start()

        pltpu.make_async_copy(g2s, g2r.at[GRP * lax.rem(me, 2) + grp], g_r.at[1]).start()

    def reduce_3():
        pltpu.make_async_copy(g2r, g2r, g_r.at[1]).wait()
        total = g2r[0]
        for e in range(1, 2 * GRP):
            total = total + g2r[e]
        g3s[...] = total
        xy_step(2, lambda e: g3s, g3r, xy)

    def reduce_4():
        pltpu.make_async_copy(g3r, g3r, g_r.at[2]).wait()
        gr_ref[...] = g3r[...]

    @pl.loop(0, 4)
    def _(c):
        for now in range(4):

            @pl.when(c == now)
            def _():
                arrive(now)
                if now == 0:
                    forward(5, ready=True)

        racc[...] = jnp.zeros_like(racc)

        @pl.when(c < 3)
        def _():
            pl.loop(0, HALF // JT)(physics)

        @pl.when(c == 3)
        def _():
            pl.loop(0, HALF // JT)(hold)
            reduce_1()
            pl.loop(0, HALF // JT)(finish)

        for now in range(4):

            @pl.when(c == now)
            def _():
                turn(now)
                if now in (1, 2):
                    back(now - 1)

    back(2)

    def unpack(n):
        lo, hi = BACK[n]
        span = brcv.at[:, pl.ds(lo, hi - lo)]
        pltpu.make_async_copy(span, span, b_r.at[n]).wait()

        @pl.loop(0, LAT)
        def _(src):
            rf[pl.ds(pl.multiple_of(src * 80 + lo, 8), hi - lo), :] = brcv[
                src, pl.ds(lo, hi - lo), :
            ].astype(F32)

    unpack(0)
    unpack(1)
    reduce_3()
    unpack(2)

    @pl.loop(0, MB // 4)
    def _(step):
        for sub in range(4):
            mm = 4 * step + sub
            rows = jnp.concatenate(
                [rf[pl.ds(MB * q + mm, LAT, stride=80), :] for q in range(4)], axis=0
            )
            t = rows.T.astype(BF16)
            a_ref[wave(mm)] = jnp.concatenate(
                [
                    jnp.concatenate([t[:32], t[64:96]], axis=0),
                    jnp.concatenate([t[32:64], t[96:]], axis=0),
                ],
                axis=1,
            )

    reduce_4()

    for n, (lo, hi) in enumerate(SEND):
        span = snd.at[pl.ds(0, LAT - 1), pl.ds(lo, hi - lo)]
        pltpu.make_async_copy(span, span, f_s.at[n]).wait()
    for n, (lo, hi) in enumerate(BACK):
        span = bsnd.at[pl.ds(0, LAT - 1), pl.ds(lo, hi - lo)]
        pltpu.make_async_copy(span, span, b_s.at[n]).wait()
    for n, count, buf in ((0, XY - 1, g1), (1, 2 * GRP - 1, g2r), (2, XY - 1, g3r)):
        span = buf.at[pl.ds(0, count)]
        pltpu.make_async_copy(span, span, g_s.at[n]).wait()


def body(
    tables,
    spectral_state, cotangent, legendre, quadrature, damping, physics_in, physics_bias, physics_out,
):
    hbm = pl.BlockSpec(memory_space=pl.ANY)
    vmem = pl.BlockSpec(memory_space=pltpu.VMEM)
    dma = pltpu.SemaphoreType.DMA
    scratch = [
        pltpu.VMEM((1, NP), F32),
        pltpu.VMEM((1, CH), F32),
        pltpu.VMEM((CH, HID), BF16),
        pltpu.VMEM((1, HID), F32),
        pltpu.VMEM((CH, HID), BF16),
        pltpu.VMEM((MB, 2 * CH, NL), BF16),
        pltpu.VMEM((MB, 2 * CH, NL), BF16),
        pltpu.VMEM((MB, NL, NP), BF16),
        pltpu.VMEM((2, HALF, COLS), BF16),
        pltpu.VMEM((CH, NL), F32),
        pltpu.VMEM((MB * NP, 128), F32),
        pltpu.VMEM((80, 128), F32),
        pltpu.VMEM((LAT, 160, 128), BF16),
        pltpu.VMEM((LAT, 160, 128), BF16),
        pltpu.VMEM((LAT * 80, 128), F32),
        pltpu.VMEM((2, COLS, 128), BF16),
        pltpu.VMEM((2, 256, 2 * HID), BF16),
        pltpu.VMEM((HALF // JT, 2, 2 * JT, HID), BF16),
        pltpu.VMEM((2, 64, COLS), F32),
        pltpu.VMEM((4 * 640, 128), F32),
        pltpu.VMEM((LAT, 80, 128), BF16),
        pltpu.VMEM((LAT, 80, 128), BF16),
        pltpu.VMEM((48, HID), F32),
        pltpu.VMEM((CH, HID), F32),
        pltpu.VMEM((XY, GR, 128), F32),
        pltpu.VMEM((XY, GR, 128), F32),
        pltpu.VMEM((GR, 128), F32),
        pltpu.VMEM((2 * GRP, GR, 128), F32),
        pltpu.VMEM((GR, 128), F32),
        pltpu.VMEM((XY, GR, 128), F32),
        dma((5,)),
        dma((3, MB)),
        dma,
        dma((6,)),
        dma((6,)),
        dma((3,)),
        dma((3,)),
        dma((3,)),
        dma((3,)),
    ]
    fourier, grads = pl.pallas_call(
        kernel,
        out_shape=[
            jax.ShapeDtypeStruct((MB, 2 * CH, NP), BF16),
            jax.ShapeDtypeStruct((XY, GR, 128), F32),
        ],
        in_specs=[hbm] * 9,
        out_specs=[vmem, vmem],
        scratch_shapes=scratch,
        compiler_params=pltpu.CompilerParams(
            collective_id=0, has_side_effects=True, vmem_limit_bytes=VMEM_LIMIT
        ),
    )(
        spectral_state[0],
        cotangent[0],
        legendre,
        tables,
        quadrature[None, :],
        damping[None, :],
        physics_in.T,
        physics_bias[None, :],
        physics_out,
    )
    whole = lambda *shape: pl.BlockSpec(shape, lambda i: (0,) * len(shape))
    part = lambda *shape: pl.BlockSpec((STEP,) + shape, lambda i: (i, 0, 0))
    grad_state, grad_in, grad_bias, grad_out = pl.pallas_call(
        inverse_kernel,
        grid=(MB // STEP,),
        out_shape=[
            jax.ShapeDtypeStruct((MB, 2 * CH, NL), F32),
            jax.ShapeDtypeStruct((CH, HID), F32),
            jax.ShapeDtypeStruct((1, HID), F32),
            jax.ShapeDtypeStruct((CH, HID), F32),
        ],
        in_specs=[
            part(2 * CH, NP),
            part(2 * CH, NL),
            part(NL, NP),
            whole(1, CH),
            whole(XY, GR, 128),
        ],
        out_specs=[part(2 * CH, NL), whole(CH, HID), whole(1, HID), whole(CH, HID)],
        scratch_shapes=[pltpu.VMEM((2 * CH, NL), F32)],
        compiler_params=pltpu.CompilerParams(vmem_limit_bytes=24 * 2**20),
    )(fourier, cotangent[0], legendre, damping[None, :], grads)
    return (grad_state[None], grad_in.T, grad_bias[0], grad_out)


def solution(mesh):
    in_specs = (
        P(),
        P("grp", "lat", None, None),
        P("grp", "lat", None, None),
        P("lat", None, None),
        P(),
        P(),
        P(),
        P(),
        P(),
    )
    out_specs = (P("grp", "lat", None, None), P(), P(), P())
    mapped = jax.shard_map(body, mesh=mesh, in_specs=in_specs, out_specs=out_specs, check_vma=False)
    tables = longitude_tables()

    def run(*args):
        return mapped(jnp.asarray(tables), *args)

    return run
```

```python
import functools
import math

import jax
import jax.numpy as jnp
import ml_dtypes
import numpy as np
from jax import lax
from jax.experimental import pallas as pl
from jax.experimental.pallas import tpu as pltpu
from jax.sharding import PartitionSpec as P

NLON = 2560
HALF = NLON // 2
MESH = pl.DeviceIdType.MESH
F32, BF16 = jnp.float32, jnp.bfloat16

LAT = 32
GRP = 8
XY = 16
MB = 20
HB = MB // 2
NL = 640
NP = 256
CH = 32
HID = 512
COLS = 640
JT = 640
SEND = ((0, 16), (16, 32), (32, 48), (48, 80), (80, 128), (128, 160))
ARRIVE = ((0, 1, 2), (3,), (4,), (5,))
BACK = ((0, 32), (32, 48), (48, 80))
GR = 17
STEP = 10
VMEM_LIMIT = 54 * 2**20


def table_rows(e):
    if e < 8:
        base = 256 * (e // 4) + LAT * (e % 4)
        return base, base + 128
    return 512 + LAT * (e - 8), 576 + LAT * (e - 8)


def longitude_tables():
    place = np.arange(HALF, dtype=np.int64)[:, None]
    owner = np.arange(LAT, dtype=np.int64)[None, :]
    tables = np.zeros((2, HALF, COLS), np.float64)
    scale = math.sqrt(2.0 / NLON)
    for parity in range(2):
        for e in range(HB):
            wave = MB * owner + 2 * e + parity
            angle = (wave * place % NLON) * (2.0 * math.pi / NLON)
            c, s = table_rows(e)
            tables[parity, :, c : c + LAT] = np.cos(angle) * scale
            tables[parity, :, s : s + LAT] = -np.sin(angle) * scale
    return tables.astype(ml_dtypes.bfloat16)


def dot(a, b, ca, cb):
    return lax.dot_general(a, b, (((ca,), (cb,)), ((), ())), preferred_element_type=F32)


def implicit_factor(damping):
    across = lax.broadcasted_iota(jnp.int32, (CH, CH), 0)
    along = lax.broadcasted_iota(jnp.int32, (CH, CH), 1)
    column = jnp.sum(jnp.where(across == along, damping, 0.0), axis=1, keepdims=True)
    degree = lax.broadcasted_iota(jnp.int32, (CH, NL), 1).astype(F32)
    ratio = degree * (degree + 1.0) / (NL * (NL + 1.0))
    return 1.0 / (1.0 + column * ratio)


def inverse_kernel(a_ref, cot_ref, leg_ref, damp_ref, gr_ref, out_ref, gi_ref, gb_ref, go_ref, fac):
    @pl.when(pl.program_id(0) == 0)
    def _():
        factor = implicit_factor(damp_ref[...])
        fac[...] = jnp.concatenate([factor, factor], axis=0)
        scale = 1.0 / math.sqrt(GRP * NP * NLON)
        for e in range(XY):
            block, tile = e // 4, e % 4
            cols = pl.ds(128 * tile, 128)
            piece = gr_ref[e, pl.ds(0, 16), :] * scale
            if block < 2:
                gi_ref[pl.ds(16 * block, 16), cols] = piece
            else:
                go_ref[pl.ds(16 * (block - 2), 16), cols] = piece
            if block == 0:
                gb_ref[:, cols] = gr_ref[e, pl.ds(16, 1), :] * scale

    for i in range(STEP):
        out_ref[i] = cot_ref[i].astype(F32) * fac[...] + dot(a_ref[i], leg_ref[i], 1, 1)


def kernel(
    spec_hbm, cot_hbm, leg_hbm, tab_hbm, quad_hbm, damp_hbm, pin_hbm, bias_hbm, pout_hbm,
    a_ref, gr_ref,
    quad_ref, damp_ref, pin_ref, bias_ref, pout_ref, spec, cot, leg, tab, factor, ft, stage, snd, rcv, rf, wdft, wp, held, racc, rall, bsnd, brcv,
    gp, ga, gsnd, g1, g2s, g2r, g3s, g3r,
    small_sem, in_sem, tab_sem, f_s, f_r, b_s, b_r, g_s, g_r,
):
    me = lax.axis_index("lat")
    grp = lax.axis_index("grp")
    xy = me // 2
    partner = me + 1 - 2 * lax.rem(me, 2)

    def peer(k):
        return lax.rem(me + k, LAT)

    barrier = pltpu.get_barrier_semaphore()

    @pl.loop(1, LAT)
    def _(k):
        pl.semaphore_signal(barrier, inc=1, device_id={"lat": peer(k)}, device_id_type=MESH)

    @pl.loop(1, GRP)
    def _(k):
        pl.semaphore_signal(
            barrier, inc=1, device_id={"grp": lax.rem(grp + k, GRP)}, device_id_type=MESH
        )

    @pl.loop(1, GRP)
    def _(k):
        pl.semaphore_signal(
            barrier,
            inc=1,
            device_id={"lat": partner, "grp": lax.rem(grp + k, GRP)},
            device_id_type=MESH,
        )

    def wave(mm):
        return 2 * lax.rem(mm, HB) + mm // HB

    def loads(mm):
        m = wave(mm)
        return [
            pltpu.make_async_copy(src.at[m], dst.at[m], in_sem.at[i, mm])
            for i, (src, dst) in enumerate(((spec_hbm, spec), (cot_hbm, cot), (leg_hbm, leg)))
        ]

    small = [
        pltpu.make_async_copy(src, dst, small_sem.at[i])
        for i, (src, dst) in enumerate(
            (
                (damp_hbm, damp_ref),
                (quad_hbm, quad_ref),
                (pin_hbm, pin_ref),
                (bias_hbm, bias_ref),
                (pout_hbm, pout_ref),
            )
        )
    ]
    for copy in small:
        copy.start()

    @pl.loop(0, MB)
    def _(mm):
        for copy in loads(mm):
            copy.start()

    tab_copy = pltpu.make_async_copy(tab_hbm, tab, tab_sem)

    for copy in small:
        copy.wait()
    factor[...] = implicit_factor(damp_ref[...])

    def legendre(mm):
        m = wave(mm)
        for copy in loads(mm):
            copy.wait()
        fac = factor[...]
        s = spec[m]
        c = cot[m].astype(F32)
        c_re = (c[:CH] * fac).astype(BF16)
        c_im = (c[CH:] * fac).astype(BF16)
        lhs = jnp.concatenate([s[:CH], c_re, s[CH:], c_im], axis=0)
        four = dot(lhs, leg[m], 1, 0)
        quad = quad_ref[...]
        four = jnp.concatenate(
            [four[:32], four[32:64] * quad, four[64:96], four[96:] * quad], axis=0
        )
        ft[pl.ds(pl.multiple_of(mm * NP, NP), NP), :] = four.T

    def tile(q, t, d):
        rows = [
            ft[pl.ds(8 * t * NP + 128 * half + 32 * q + d, 8, stride=NP), :] for half in range(2)
        ]
        return jnp.concatenate(rows, axis=0).astype(BF16)

    def rest(pair, d):
        for j in range(4):
            row = 16 * NP + 128 * (j % 2) + 32 * (2 * pair + j // 2) + d
            stage[pl.ds(4 * j, 4), :] = ft[pl.ds(row, 4, stride=NP), :]
        return stage[pl.ds(0, 16), :].astype(BF16)

    def assemble(n, d):
        if n < 2:
            snd[d, pl.ds(16 * n, 16), :] = tile(0, n, d)
        elif n == 2:
            snd[d, pl.ds(32, 16), :] = rest(0, d)
        elif n == 3:
            for t in range(2):
                snd[d, pl.ds(48 + 16 * t, 16), :] = tile(1, t, d)
        elif n == 4:
            for t in range(2):
                snd[d, pl.ds(80 + 16 * t, 16), :] = tile(2, t, d)
            snd[d, pl.ds(112, 16), :] = rest(1, d)
        else:
            for t in range(2):
                snd[d, pl.ds(128 + 16 * t, 16), :] = tile(3, t, d)

    def send(n, d):
        lo, hi = SEND[n]
        pltpu.make_async_remote_copy(
            src_ref=snd.at[d, pl.ds(lo, hi - lo)],
            dst_ref=rcv.at[me, pl.ds(lo, hi - lo)],
            send_sem=f_s.at[n],
            recv_sem=f_r.at[n],
            device_id={"lat": d},
            device_id_type=MESH,
        ).start()

    def far(f):
        @pl.loop(0, LAT // 2)
        def _(i):
            f(peer(2 * i + 1))

    def near(f):
        @pl.loop(1, LAT // 2)
        def _(i):
            f(peer(2 * i))

    def far_then_near(f):
        far(f)
        near(f)

    def forward(n, ready=False):
        def f(d):
            if not ready:
                assemble(n, d)
            send(n, d)

        far_then_near(f)
        if not ready:
            assemble(n, me)
        lo, hi = SEND[n]
        pltpu.make_async_copy(
            snd.at[me, pl.ds(lo, hi - lo)], rcv.at[me, pl.ds(lo, hi - lo)], f_r.at[n]
        ).start()

    pl.loop(0, 8)(legendre)
    pl.semaphore_wait(barrier, LAT - 1 + 2 * (GRP - 1))
    forward(0)
    pl.loop(8, 16)(legendre)
    forward(1)
    pl.loop(16, MB)(legendre)
    tab_copy.start()
    forward(2)
    forward(3)
    forward(4)

    @pl.loop(0, LAT)
    def _(d):
        assemble(5, d)

    wp[...] = jnp.zeros_like(wp)
    half_in = (0.5 * pin_ref[...].astype(F32)).astype(BF16)
    half_out = (0.5 * pout_ref[...].astype(F32)).astype(BF16)
    half_bias = 0.5 * bias_ref[...]
    top = half_bias.astype(BF16).astype(F32)
    mid = (half_bias - top).astype(BF16).astype(F32)
    low = half_bias - top - mid
    row = lax.broadcasted_iota(jnp.int32, (16, HID), 0)
    bias_rows = jnp.where(
        row == 0, top, jnp.where(row == 1, mid, jnp.where(row == 2, low, 0.0))
    ).astype(BF16)
    for s in range(2):
        wp[s, pl.ds(64 * s, CH), pl.ds(0, HID)] = half_in
        wp[s, pl.ds(64 * s + CH, CH), pl.ds(HID, HID)] = half_out
        wp[s, pl.ds(128, 16), pl.ds(0, HID)] = bias_rows
    gp[...] = jnp.zeros_like(gp)
    ga[...] = jnp.zeros_like(ga)
    tab_copy.wait()

    lane = lax.broadcasted_iota(jnp.int32, (LAT, 128), 1)
    left = lane < 64

    def arrive(c):
        for n in ARRIVE[c]:
            lo, hi = SEND[n]
            span = rcv.at[:, pl.ds(lo, hi - lo)]
            pltpu.make_async_copy(span, span, f_r.at[n]).wait()
            at = lo % 80

            @pl.loop(0, LAT)
            def _(src):
                rf[pl.ds(pl.multiple_of(src * 80 + at, 8), hi - lo), :] = rcv[
                    src, pl.ds(lo, hi - lo), :
                ].astype(F32)

        def row(half, mm):
            if mm < 16:
                return 48 * (c % 2) + 16 * (mm // 8) + 8 * half + mm % 8
            return 32 + 8 * (c % 2) + 4 * half + mm - 16

        for mm in range(MB):
            w0 = rf[pl.ds(row(0, mm), LAT, stride=80), :]
            w1 = rf[pl.ds(row(1, mm), LAT, stride=80), :]
            re = jnp.where(left, w0, pltpu.roll(w1, 64, 1))
            im = jnp.where(left, pltpu.roll(w0, 64, 1), w1)
            r_re, r_im = table_rows(mm % HB)
            wdft[mm // HB, pl.ds(r_re, LAT), :] = re.astype(BF16)
            wdft[mm // HB, pl.ds(r_im, LAT), :] = im.astype(BF16)

    one_lane = lax.broadcasted_iota(jnp.int32, (2 * JT, 128), 1)
    ones = jnp.where(one_lane < 3, 1.0, 0.0).astype(BF16)
    ones_t = jnp.ones((16, 2 * JT), BF16)

    def columns(i, grid_gradient):
        span = pl.ds(pl.multiple_of(i * JT, JT), JT)
        even = dot(tab[0, span, :], wdft[0], 1, 0)
        odd = dot(tab[1, span, :], wdft[1], 1, 0)
        x = jnp.concatenate([(even + odd).astype(BF16), (even - odd).astype(BF16)], axis=0)
        xe = jnp.concatenate([x, ones], axis=1)
        xt = x.T
        grads = []
        for s in range(2):
            h = dot(xe, wp[s, :, pl.ds(0, HID)], 1, 0)
            u = dot(xe, wp[s, :, pl.ds(HID, HID)], 1, 0)
            a = 1.0 + jnp.tanh(h)
            act = h * a
            pre = (u * (a * ((1.0 + (h + h)) - act))).astype(BF16)
            act = act.astype(BF16)
            grads.append(grid_gradient(s, pre))
            lhs = jnp.concatenate([xt[64 * s : 64 * s + CH], ones_t], axis=0)
            gp[...] += dot(lhs, pre, 1, 0)
            ga[...] += dot(xt[64 * s + CH : 64 * s + 64], act, 1, 0)
        return grads

    def longitudes(i, grads):
        span = pl.ds(pl.multiple_of(i * JT, JT), JT)
        gg = jnp.concatenate(grads, axis=0)
        g_even = (gg[:, :JT] + gg[:, JT:]).astype(BF16)
        g_odd = (gg[:, :JT] - gg[:, JT:]).astype(BF16)
        racc[0] += dot(g_even, tab[0, span, :], 1, 0)
        racc[1] += dot(g_odd, tab[1, span, :], 1, 0)

    def physics(i):
        longitudes(i, columns(i, lambda s, pre: dot(pin_ref[...], pre, 1, 1)))

    def hold(i):
        def keep(s, pre):
            held[i, s] = pre

        columns(i, keep)

    def finish(i):
        longitudes(i, [dot(pin_ref[...], held[i, s], 1, 1) for s in range(2)])

    def turn(c):
        for parity in range(2):
            r = racc[parity]
            base = 640 * c + 320 * parity
            rall[pl.ds(base, 128), :] = jnp.concatenate([r[:, :128], r[:, 128:256]], axis=0).T
            rall[pl.ds(base + 128, 128), :] = jnp.concatenate(
                [r[:, 256:384], r[:, 384:512]], axis=0
            ).T
            last = r[:, 512:]
            both = jnp.concatenate([last, pltpu.roll(last, 64, 1)], axis=0).T
            rall[pl.ds(base + 256, 64), :] = both[:64]

    def pack(n, d):
        lo, hi = BACK[n]
        for q in range(lo // MB, (hi - 1) // MB + 1):
            stage[pl.ds(MB * q, MB), :] = rall[pl.ds(640 * q + d, MB, stride=LAT), :]
        bsnd[d, pl.ds(lo, hi - lo), :] = stage[pl.ds(lo, hi - lo), :].astype(BF16)

    def back(n):
        lo, hi = BACK[n]

        def go(d):
            pack(n, d)
            go_packed(d)

        def go_packed(d):
            pltpu.make_async_remote_copy(
                src_ref=bsnd.at[d, pl.ds(lo, hi - lo)],
                dst_ref=brcv.at[me, pl.ds(lo, hi - lo)],
                send_sem=b_s.at[n],
                recv_sem=b_r.at[n],
                device_id={"lat": d},
                device_id_type=MESH,
            ).start()

        if n < 2:
            far_then_near(go)
        else:
            near(go)
        pack(n, me)
        pltpu.make_async_copy(
            bsnd.at[me, pl.ds(lo, hi - lo)], brcv.at[me, pl.ds(lo, hi - lo)], b_r.at[n]
        ).start()
        if n == 2:
            pl.loop(0, LAT // 2)(lambda i: pack(n, peer(2 * i + 1)))
            reduce_2()
            far(go_packed)

    def xy_step(n, src, dst, mine):
        @pl.loop(1, XY)
        def _(i):
            d = peer(2 * i)
            pltpu.make_async_remote_copy(
                src_ref=src(d // 2),
                dst_ref=dst.at[xy],
                send_sem=g_s.at[n],
                recv_sem=g_r.at[n],
                device_id={"lat": d},
                device_id_type=MESH,
            ).start()

        pltpu.make_async_copy(src(mine), dst.at[xy], g_r.at[n]).start()

    def reduce_1():
        for e in range(XY):
            block, tile = e // 4, e % 4
            cols = pl.ds(128 * tile, 128)
            if block < 2:
                gsnd[e, pl.ds(0, 16), :] = gp[pl.ds(16 * block, 16), cols]
            else:
                gsnd[e, pl.ds(0, 16), :] = ga[pl.ds(16 * (block - 2), 16), cols]
            gsnd[e, pl.ds(16, 1), :] = gp[pl.ds(CH, 1), cols]
        xy_step(0, lambda e: gsnd.at[e], g1, xy)

    def reduce_2():
        pltpu.make_async_copy(g1, g1, g_r.at[0]).wait()
        total = g1[0]
        for e in range(1, XY):
            total = total + g1[e]
        g2s[...] = total

        for far in (1, 0):

            @pl.loop(1 - far, GRP)
            def _(k):
                pltpu.make_async_remote_copy(
                    src_ref=g2s,
                    dst_ref=g2r.at[GRP * lax.rem(me, 2) + grp],
                    send_sem=g_s.at[1],
                    recv_sem=g_r.at[1],
                    device_id={
                        "lat": partner if far else me,
                        "grp": lax.rem(grp + k, GRP),
                    },
                    device_id_type=MESH,
                ).start()

        pltpu.make_async_copy(g2s, g2r.at[GRP * lax.rem(me, 2) + grp], g_r.at[1]).start()

    def reduce_3():
        pltpu.make_async_copy(g2r, g2r, g_r.at[1]).wait()
        total = g2r[0]
        for e in range(1, 2 * GRP):
            total = total + g2r[e]
        g3s[...] = total
        xy_step(2, lambda e: g3s, g3r, xy)

    def reduce_4():
        pltpu.make_async_copy(g3r, g3r, g_r.at[2]).wait()
        gr_ref[...] = g3r[...]

    @pl.loop(0, 4)
    def _(c):
        for now in range(4):

            @pl.when(c == now)
            def _():
                arrive(now)
                if now == 0:
                    forward(5, ready=True)

        racc[...] = jnp.zeros_like(racc)

        @pl.when(c < 3)
        def _():
            pl.loop(0, HALF // JT)(physics)

        @pl.when(c == 3)
        def _():
            pl.loop(0, HALF // JT)(hold)
            reduce_1()
            pl.loop(0, HALF // JT)(finish)

        for now in range(4):

            @pl.when(c == now)
            def _():
                turn(now)
                if now in (1, 2):
                    back(now - 1)

    back(2)

    def unpack(n):
        lo, hi = BACK[n]
        span = brcv.at[:, pl.ds(lo, hi - lo)]
        pltpu.make_async_copy(span, span, b_r.at[n]).wait()

        @pl.loop(0, LAT)
        def _(src):
            rf[pl.ds(pl.multiple_of(src * 80 + lo, 8), hi - lo), :] = brcv[
                src, pl.ds(lo, hi - lo), :
            ].astype(F32)

    unpack(0)
    unpack(1)
    reduce_3()
    unpack(2)

    @pl.loop(0, MB // 4)
    def _(step):
        for sub in range(4):
            mm = 4 * step + sub
            rows = jnp.concatenate(
                [rf[pl.ds(MB * q + mm, LAT, stride=80), :] for q in range(4)], axis=0
            )
            t = rows.T.astype(BF16)
            a_ref[wave(mm)] = jnp.concatenate(
                [
                    jnp.concatenate([t[:32], t[64:96]], axis=0),
                    jnp.concatenate([t[32:64], t[96:]], axis=0),
                ],
                axis=1,
            )

    reduce_4()

    for n, (lo, hi) in enumerate(SEND):
        span = snd.at[pl.ds(0, LAT - 1), pl.ds(lo, hi - lo)]
        pltpu.make_async_copy(span, span, f_s.at[n]).wait()
    for n, (lo, hi) in enumerate(BACK):
        span = bsnd.at[pl.ds(0, LAT - 1), pl.ds(lo, hi - lo)]
        pltpu.make_async_copy(span, span, b_s.at[n]).wait()
    for n, count, buf in ((0, XY - 1, g1), (1, 2 * GRP - 1, g2r), (2, XY - 1, g3r)):
        span = buf.at[pl.ds(0, count)]
        pltpu.make_async_copy(span, span, g_s.at[n]).wait()


def body(
    tables,
    spectral_state, cotangent, legendre, quadrature, damping, physics_in, physics_bias, physics_out,
):
    hbm = pl.BlockSpec(memory_space=pl.ANY)
    vmem = pl.BlockSpec(memory_space=pltpu.VMEM)
    dma = pltpu.SemaphoreType.DMA
    scratch = [
        pltpu.VMEM((1, NP), F32),
        pltpu.VMEM((1, CH), F32),
        pltpu.VMEM((CH, HID), BF16),
        pltpu.VMEM((1, HID), F32),
        pltpu.VMEM((CH, HID), BF16),
        pltpu.VMEM((MB, 2 * CH, NL), BF16),
        pltpu.VMEM((MB, 2 * CH, NL), BF16),
        pltpu.VMEM((MB, NL, NP), BF16),
        pltpu.VMEM((2, HALF, COLS), BF16),
        pltpu.VMEM((CH, NL), F32),
        pltpu.VMEM((24 * NP, 128), F32),
        pltpu.VMEM((96, 128), F32),
        pltpu.VMEM((LAT, 160, 128), BF16),
        pltpu.VMEM((LAT, 160, 128), BF16),
        pltpu.VMEM((LAT * 80, 128), F32),
        pltpu.VMEM((2, COLS, 128), BF16),
        pltpu.VMEM((2, 256, 2 * HID), BF16),
        pltpu.VMEM((HALF // JT, 2, 2 * JT, HID), BF16),
        pltpu.VMEM((2, 64, COLS), F32),
        pltpu.VMEM((4 * 640 + 256, 128), F32),
        pltpu.VMEM((LAT, 80, 128), BF16),
        pltpu.VMEM((LAT, 80, 128), BF16),
        pltpu.VMEM((48, HID), F32),
        pltpu.VMEM((CH, HID), F32),
        pltpu.VMEM((XY, GR, 128), F32),
        pltpu.VMEM((XY, GR, 128), F32),
        pltpu.VMEM((GR, 128), F32),
        pltpu.VMEM((2 * GRP, GR, 128), F32),
        pltpu.VMEM((GR, 128), F32),
        pltpu.VMEM((XY, GR, 128), F32),
        dma((5,)),
        dma((3, MB)),
        dma,
        dma((6,)),
        dma((6,)),
        dma((3,)),
        dma((3,)),
        dma((3,)),
        dma((3,)),
    ]
    fourier, grads = pl.pallas_call(
        kernel,
        out_shape=[
            jax.ShapeDtypeStruct((MB, 2 * CH, NP), BF16),
            jax.ShapeDtypeStruct((XY, GR, 128), F32),
        ],
        in_specs=[hbm] * 9,
        out_specs=[vmem, vmem],
        scratch_shapes=scratch,
        compiler_params=pltpu.CompilerParams(
            collective_id=0, has_side_effects=True, vmem_limit_bytes=VMEM_LIMIT
        ),
    )(
        spectral_state[0],
        cotangent[0],
        legendre,
        tables,
        quadrature[None, :],
        damping[None, :],
        physics_in.T,
        physics_bias[None, :],
        physics_out,
    )
    whole = lambda *shape: pl.BlockSpec(shape, lambda i: (0,) * len(shape))
    part = lambda *shape: pl.BlockSpec((STEP,) + shape, lambda i: (i, 0, 0))
    grad_state, grad_in, grad_bias, grad_out = pl.pallas_call(
        inverse_kernel,
        grid=(MB // STEP,),
        out_shape=[
            jax.ShapeDtypeStruct((MB, 2 * CH, NL), F32),
            jax.ShapeDtypeStruct((CH, HID), F32),
            jax.ShapeDtypeStruct((1, HID), F32),
            jax.ShapeDtypeStruct((CH, HID), F32),
        ],
        in_specs=[
            part(2 * CH, NP),
            part(2 * CH, NL),
            part(NL, NP),
            whole(1, CH),
            whole(XY, GR, 128),
        ],
        out_specs=[part(2 * CH, NL), whole(CH, HID), whole(1, HID), whole(CH, HID)],
        scratch_shapes=[pltpu.VMEM((2 * CH, NL), F32)],
        compiler_params=pltpu.CompilerParams(vmem_limit_bytes=24 * 2**20),
    )(fourier, cotangent[0], legendre, damping[None, :], grads)
    return (grad_state[None], grad_in.T, grad_bias[0], grad_out)


def solution(mesh):
    in_specs = (
        P(),
        P("grp", "lat", None, None),
        P("grp", "lat", None, None),
        P("lat", None, None),
        P(),
        P(),
        P(),
        P(),
        P(),
    )
    out_specs = (P("grp", "lat", None, None), P(), P(), P())
    mapped = jax.shard_map(body, mesh=mesh, in_specs=in_specs, out_specs=out_specs, check_vma=False)
    tables = longitude_tables()

    def run(*args):
        return mapped(jnp.asarray(tables), *args)

    return run
```
